32 devices in a mesh: req: 8 (over y, x, core), seq: 4 (over z).
Axes of the slice: x: 2, y: 2, z: 4, core: 2. Of those that a mesh axis runs over, the one named last changes fastest.
Arguments:
- qkv_proj: bfloat16 [8, 512, 4096], P('req', 'seq'), may hold values from -6 to 6
- gate_proj: bfloat16 [8, 512, 2048], P('req', 'seq'), may hold values from -6 to 6
- residual: bfloat16 [8, 512, 2048], P('req', 'seq'), may hold values from -6 to 6
- log_decay: float32 [8, 512, 8], P('req', 'seq'), may hold values from -1 to 0, as said below
- beta_logit: bfloat16 [8, 512, 8], P('req', 'seq'), may hold values from -6 to 6
- lengths: int32 [8], replicated, may hold values from 1 to 512, 2048 in all
- slot_request: int32 [8], replicated, may hold values from 0 to 7, each once
- conv_weight: float32 [4, 4096], replicated, may hold values from -3 to 3
- norm_gain: float32 [256], replicated, may hold values from 0.1 to 1.9
- out_weight: bfloat16 [2048, 2048], P(('req', 'seq')), may hold values from -0.125 to 0.125
- mlp_gain: float32 [2048], replicated, may hold values from 0.1 to 1.9
- w_gate: bfloat16 [2048, 5632], P('req', 'seq'), may hold values from -0.125 to 0.125
- w_up: bfloat16 [2048, 5632], P('req', 'seq'), may hold values from -0.125 to 0.125
- w_down: bfloat16 [5632, 2048], P('seq', 'req'), may hold values from -0.078125 to 0.078125
Outputs:
- hidden_out: bfloat16 [8, 512, 2048], P('req', 'seq')
- final_state: float32 [8, 8, 128, 256], P('req', 'seq')
- conv_edge: bfloat16 [8, 3, 4096], P('req', None, 'seq')
The draws below stay inside these ranges and needn't reach their ends.
Inputs may be any that keep to these rules, and one draw needn't show every extreme that they name: Slot s of the req axis holds request slot_request[s]. The 8 lengths sum to 2048, and the longest is exactly 512. `log_decay`: every entry is negative.
All inputs are finite; a program needn't handle non-finite values.
Results may differ from the reference program's by a relative error of at most 0.014.
Values may be sent and summed in bfloat16 or wider, within the bound.
No kernel may reach another device: no remote copies, remote signals or barrier semaphores. Data moves between devices by JAX's collectives and lax.ppermute only.
A program may use at most 128 MiB of HBM per device.

```python
import math
import jax
import jax.numpy as jnp
import numpy as np
from jax import lax

D = 2048
LOCAL_HEADS = 8
DK = 128
DV = 256
FF = 5632
CONV = 4
PIECE = 128
SLOT_POSITIONS = 512
REQUEST_COUNT = 8
HK = 1024
HV = 2048
CH = 4096
TOTAL = 2048
N_SEQ = 4


def draw_log_decay(key, part):
    request_lanes = jax.random.split(key, 7)
    slow_share = 0.5
    slow_heads = jax.random.uniform(request_lanes[0], (LOCAL_HEADS,)) < slow_share
    fast_rate = -jnp.exp(jax.random.uniform(request_lanes[1], (LOCAL_HEADS,), minval=math.log(1.0 / 50.0), maxval=math.log(1.0 / 30.0)))
    slow_rate = math.log(0.1) / SLOT_POSITIONS * jax.random.uniform(request_lanes[2], (LOCAL_HEADS,), minval=0.3, maxval=1.0)
    head_decay_speed = jnp.where(slow_heads, slow_rate, fast_rate)
    piece_count = SLOT_POSITIONS // PIECE
    segment_multiplier = jnp.exp2(jax.random.uniform(request_lanes[3], (REQUEST_COUNT, piece_count, 1, LOCAL_HEADS), minval=-0.5, maxval=0.5))
    segment_multiplier = jnp.broadcast_to(segment_multiplier, (REQUEST_COUNT, piece_count, PIECE, LOCAL_HEADS)).reshape(REQUEST_COUNT, SLOT_POSITIONS, LOCAL_HEADS)
    jaggedness = jax.random.uniform(request_lanes[4], (REQUEST_COUNT, SLOT_POSITIONS, LOCAL_HEADS), minval=0.5, maxval=1.5)
    token_clusters = jax.random.uniform(request_lanes[5], (REQUEST_COUNT, SLOT_POSITIONS, LOCAL_HEADS)) < 3.0 / SLOT_POSITIONS
    cluster_length = jnp.log(jax.random.uniform(request_lanes[6], (REQUEST_COUNT, SLOT_POSITIONS, LOCAL_HEADS), minval=0.5, maxval=0.8))
    return (head_decay_speed * segment_multiplier * jaggedness + jnp.where(token_clusters, cluster_length, 0.0)).astype(jnp.float32)


def shard_levels(key, dims, cuts, low, top_value):
    def one(dim, blocks):
        draws = jax.random.uniform(jax.random.fold_in(jax.random.fold_in(key, 6), dim), (blocks,), jnp.float32, low / len(cuts), top_value / len(cuts))
        return jnp.repeat(jnp.exp(draws), dims[dim] // blocks).reshape((-1,) + (1,) * (len(dims) - dim - 1))

    loudness = one(*cuts[0])
    for cut in cuts[1:]:
        loudness = loudness * one(*cut)
    return loudness


def length_profile(amount, total, reach, lean):
    portions = [(1 << 20) // math.isqrt(grade ** lean) + 1 for grade in range(2, amount + 1)]
    rest, holding = total - reach - (amount - 1), [1] * (amount - 1)
    while rest > 0:
        candidates = [i for i in range(amount - 1) if holding[i] < reach]
        mass, left = sum([portions[i] for i in candidates]), rest
        for i in candidates:
            extra = min(reach - holding[i], max(1, left * portions[i] // mass), rest)
            holding[i] = holding[i] + extra
            rest = rest - extra
    return np.array([reach] + holding)


def ragged(stream_key, number_of, total, limit, skew):
    if number_of == 2:
        one = jax.random.randint(stream_key, (), max(1, total - limit), min(limit, total - 1) + 1)
        return jnp.stack([one, total - one])
    tallies = jnp.asarray(length_profile(number_of, total, limit, skew), jnp.int32)
    twos = (number_of - 1) // 2
    source_of, taker = tallies[1:1 + 2 * twos:2], tallies[2:2 + 2 * twos:2]
    margin = jnp.minimum(source_of - 1, limit - taker)
    passed = jax.random.randint(jax.random.fold_in(stream_key, 1), (twos,), 0, 1 << 20) % (margin + 1)
    tallies = tallies.at[1:1 + 2 * twos:2].set(source_of - passed).at[2:2 + 2 * twos:2].set(taker + passed)
    return tallies[jax.random.permutation(jax.random.fold_in(stream_key, 2), number_of)]


def gaussian(rng, shape, scale, most, cuts=(), held_as=jnp.bfloat16):
    loudness = shard_levels(rng, shape, cuts, -0.22, 0.18) if cuts else 1.0
    entries = jax.random.normal(rng, shape, jnp.float32) * scale * loudness
    return jnp.minimum(jnp.maximum(entries, -most), most).astype(held_as)


def setup_inputs(seed: int = 0) -> dict:
    arg_keys = jax.random.split(jax.random.key(seed), 15)
    return {
        "qkv_proj": gaussian(arg_keys[0], (REQUEST_COUNT, SLOT_POSITIONS, CH), 1.0, 6.0, ((0, 8), (1, 4))),
        "gate_proj": gaussian(arg_keys[1], (REQUEST_COUNT, SLOT_POSITIONS, HV), 1.0, 6.0, ((0, 8), (1, 4))),
        "residual": gaussian(arg_keys[2], (REQUEST_COUNT, SLOT_POSITIONS, D), 1.0, 6.0, ((0, 8), (1, 4))),
        "log_decay": draw_log_decay(jax.random.fold_in(arg_keys[14], 71), 0),
        "beta_logit": gaussian(arg_keys[4], (REQUEST_COUNT, SLOT_POSITIONS, LOCAL_HEADS), 1.5, 6.0, ((0, 8), (1, 4))),
        "lengths": ragged(arg_keys[5], REQUEST_COUNT, TOTAL, SLOT_POSITIONS, 2).astype(jnp.int32),
        "slot_request": jax.random.permutation(arg_keys[6], REQUEST_COUNT).astype(jnp.int32),
        "conv_weight": gaussian(arg_keys[7], (CONV, CH), 0.5, 3.0, (), jnp.float32),
        "norm_gain": jnp.clip(1.0 + 0.18 * jax.random.normal(arg_keys[8], (DV,), jnp.float32), 0.1, 1.9),
        "out_weight": gaussian(arg_keys[9], (HV, D), HV ** -0.5, 0.125, ((0, 32),)),
        "mlp_gain": jnp.clip(1.0 + 0.18 * jax.random.normal(arg_keys[10], (D,), jnp.float32), 0.1, 1.9),
        "w_gate": gaussian(arg_keys[11], (D, FF), D ** -0.5, 0.125, ((0, 8), (1, 4))),
        "w_up": gaussian(arg_keys[12], (D, FF), D ** -0.5, 0.125, ((0, 8), (1, 4))),
        "w_down": gaussian(arg_keys[13], (FF, D), FF ** -0.5, 0.078125, ((0, 4), (1, 8))),
    }


EPS_NORM = 1e-05
EPS_UNIT = 1e-06
HIGHEST = lax.Precision.HIGHEST

def unit_norm(vector):
    return vector * lax.rsqrt(lax.optimization_barrier(jnp.sum(vector * vector, axis=-1, keepdims=True)) + EPS_UNIT)

def reference(qkv_proj, gate_proj, residual, log_decay, beta_logit, lengths, slot_request, conv_weight, norm_gain, out_weight, mlp_gain, w_gate, w_up, w_down):
    slot_length = jnp.take(lengths, slot_request)
    position = jnp.arange(SLOT_POSITIONS, dtype=jnp.int32)
    live_mask = position[None, :] < slot_length[:, None]
    inputs = qkv_proj.astype(jnp.float32)
    padded = jnp.pad(inputs, ((0, 0), (CONV - 1, 0), (0, 0)))
    convolved = jnp.zeros_like(inputs)
    for offset in range(CONV):
        convolved = convolved + conv_weight[offset] * padded[:, offset:offset + SLOT_POSITIONS]
    activated = jax.nn.silu(convolved)
    query_vec = unit_norm(activated[..., :HK].reshape(REQUEST_COUNT, SLOT_POSITIONS, LOCAL_HEADS, DK)) * DK ** (-0.5)
    key_vecs = unit_norm(activated[..., HK:2 * HK].reshape(REQUEST_COUNT, SLOT_POSITIONS, LOCAL_HEADS, DK))
    values = activated[..., 2 * HK:].reshape(REQUEST_COUNT, SLOT_POSITIONS, LOCAL_HEADS, DV)
    beta_gate = jax.nn.sigmoid(beta_logit.astype(jnp.float32)) * live_mask[..., None]
    decay_rate = jnp.exp(jnp.where(live_mask[..., None], log_decay, 0.0))

    def advance(carry_state, inputs_now):
        query_now, keys_now, values_now, beta_now, decay_now = inputs_now
        projected = jnp.einsum('rhk,rhkv->rhv', keys_now, carry_state, precision=HIGHEST)
        rank_one = beta_now[..., None, None] * keys_now[..., :, None]
        carry_state = decay_now[..., None, None] * (carry_state - rank_one * projected[..., None, :]) + rank_one * values_now[..., None, :]
        output_now = jnp.einsum('rhk,rhkv->rhv', query_now, carry_state, precision=HIGHEST)
        return (carry_state, output_now)
    sequence = tuple((jnp.moveaxis(tensor, 1, 0) for tensor in (query_vec, key_vecs, values, beta_gate, decay_rate)))
    initial = jnp.zeros((REQUEST_COUNT, LOCAL_HEADS, DK, DV), jnp.float32)
    final_state, outputs = lax.scan(advance, initial, sequence)
    outputs = jnp.moveaxis(outputs, 0, 1)
    edge_index = slot_length[:, None] - (CONV - 1) + jnp.arange(CONV - 1, dtype=jnp.int32)[None, :]
    taken = jnp.take_along_axis(qkv_proj, jnp.clip(edge_index, 0, SLOT_POSITIONS - 1)[:, :, None], axis=1)
    conv_edge = jnp.where((edge_index >= 0)[:, :, None], taken, jnp.zeros_like(taken))
    gate_values = gate_proj.astype(jnp.float32).reshape(REQUEST_COUNT, SLOT_POSITIONS, LOCAL_HEADS, DV)
    scaled = outputs * lax.rsqrt(lax.optimization_barrier(jnp.mean(outputs * outputs, axis=-1, keepdims=True)) + EPS_NORM)
    mixed_heads = (scaled * norm_gain * jax.nn.silu(gate_values)).reshape(REQUEST_COUNT, SLOT_POSITIONS, HV).astype(jnp.bfloat16)
    shard_width = FF // N_SEQ

    def finish(request_items):
        mixed_rows, residual_rows, live_rows = request_items
        attended = jnp.dot(mixed_rows, out_weight, preferred_element_type=jnp.float32)
        hidden_state = (residual_rows.astype(jnp.float32) + attended).astype(jnp.bfloat16)
        stream = hidden_state.astype(jnp.float32)
        normed = (stream * lax.rsqrt(lax.optimization_barrier(jnp.mean(stream * stream, axis=-1, keepdims=True)) + EPS_NORM) * mlp_gain).astype(jnp.bfloat16)
        gate_part = jnp.dot(normed, w_gate, preferred_element_type=jnp.float32)
        upward = jnp.dot(normed, w_up, preferred_element_type=jnp.float32)
        inner_units = (jax.nn.silu(gate_part) * upward).astype(jnp.bfloat16)
        combined = stream
        for shard_index in range(N_SEQ):
            lower_edge = shard_index * shard_width
            partial_value = jnp.dot(inner_units[:, lower_edge:lower_edge + shard_width], w_down[lower_edge:lower_edge + shard_width], preferred_element_type=jnp.float32)
            combined = combined + lax.optimization_barrier(partial_value.astype(jnp.bfloat16)).astype(jnp.float32)
        return jnp.where(live_rows[:, None], combined, 0.0).astype(jnp.bfloat16)
    hidden_out = lax.map(finish, (mixed_heads, residual, live_mask))
    return (hidden_out, final_state, conv_edge)
```

```python
import functools

import jax
import jax.numpy as jnp
from jax import lax
from jax.experimental import pallas as pl
from jax.experimental.pallas import tpu as pltpu
from jax.sharding import PartitionSpec as P

HEADS = 8
DK = 128
DV = 256
CONV = 4
HK = HEADS * DK
EPS_NORM = 1e-05
EPS_UNIT = 1e-06
BF16 = jnp.bfloat16
F32 = jnp.float32
MIB = 1 << 20

VMEM = pl.BlockSpec(memory_space=pltpu.VMEM)
SMEM = pl.BlockSpec(memory_space=pltpu.SMEM)
ANY = pl.BlockSpec(memory_space=pl.ANY)


def dot(a, b):
    return jnp.dot(a.astype(BF16), b.astype(BF16), preferred_element_type=F32)


def dot_nt(a, b):
    return lax.dot_general(
        a.astype(BF16), b.astype(BF16), (((1,), (1,)), ((), ())), preferred_element_type=F32
    )


def silu(v):
    return v / (1.0 + jnp.exp(-v))


def shift(value, axis, count, steps):
    return lax.ppermute(value, axis, [(i, (i + steps) % count) for i in range(count)])


def flip(value, bits):
    return lax.ppermute(value, "req", [(i, i ^ bits) for i in range(lax.axis_size("req"))])


def cubic():
    return lax.axis_size("req") == 8


def gather_req(block, axis):
    if not cubic():
        return [lax.all_gather(block, "req", axis=axis, tiled=True)]
    half = block.shape[axis] // 2
    by_two, by_four = flip(block, 2), flip(block, 4)
    low = flip(lax.slice_in_dim(by_two, 0, half, axis=axis), 4)
    high = flip(lax.slice_in_dim(by_four, half, 2 * half, axis=axis), 2)
    mine = [[block], [by_two], [by_four], [low, high]]
    theirs = [[flip(part, 1) for part in parts] for parts in mine]
    out = []
    for a, b in zip(mine, theirs):
        out += [a, b]
    return out


def delta_kernel(count, heads, piece, *refs):
    x_refs, small_refs = refs[:count], refs[count : 2 * count]
    where, taps, gain = refs[2 * count : 2 * count + 3]
    attn, state, xs, bs = refs[2 * count + 3 :]
    me = where[0]
    q0, k0, v0 = 0, heads * DK, 2 * heads * DK
    xs[pl.ds(0, 8), :] = jnp.zeros((8, xs.shape[1]), F32)
    for k in range(count):
        c = lax.rem(me - k + count, count)
        xs[pl.ds(pl.multiple_of(8 + c * piece, 8), piece), :] = x_refs[k][...].astype(F32)
        bs[c] = small_refs[k][0:8, :]

    def activated(c, col, width):
        total = None
        for i in range(CONV):
            rows = xs[pl.ds(8 - (CONV - 1) + i + c * piece, piece), pl.ds(col, width)]
            term = taps[i : i + 1, col : col + width] * rows
            total = term if total is None else total + term
        return silu(total)

    def unit(v):
        return v * lax.rsqrt(jnp.sum(v * v, axis=-1, keepdims=True) + EPS_UNIT)

    row = lax.broadcasted_iota(jnp.int32, (piece, piece), 0)
    col = lax.broadcasted_iota(jnp.int32, (piece, piece), 1)
    upper = (row <= col).astype(F32)
    pairs = [(c, h) for c in range(count) for h in range(heads)]
    tabs = {}
    for c in range(count):
        rows = bs[c]
        cum = jnp.dot(rows, upper, precision=lax.Precision.HIGHEST, preferred_element_type=F32)
        wide = jnp.concatenate([cum, rows, jnp.zeros((piece - 16, piece), F32)], axis=0)
        tall = wide.T
        for h in range(heads):
            g_row = cum[heads + h : heads + h + 1, :]
            g_col = tall[:, heads + h : heads + h + 1]
            b_col = tall[:, 8 + h : 9 + h]
            tabs[c, h] = (g_row, g_col, b_col)
    couple, solve, first, second, ends = {}, {}, {}, {}, {}
    for c, h in pairs:
        g_row, g_col, b_col = tabs[c, h]
        q = unit(activated(c, q0 + h * DK, DK)) * DK ** (-0.5)
        k = unit(activated(c, k0 + h * DK, DK))
        v = activated(c, v0 + h * DV, DV)
        inner = dot_nt(jnp.concatenate([k, q], axis=0), k)
        spread = jnp.exp(jnp.where(row >= col, g_col - g_row, -1e30))
        couple[c, h] = jnp.where(row > col, inner[:piece] * spread * b_col, 0.0)
        grown = jnp.exp(g_col)
        g_end = g_row[:, piece - 1 : piece]
        to_end = jnp.exp(g_end - g_col) * k
        solve[c, h] = jnp.concatenate([b_col * v, (b_col * grown) * k], axis=1).astype(BF16)
        first[c, h] = (grown * q).astype(BF16)
        second[c, h] = jnp.concatenate([inner[piece:] * spread, to_end.T], axis=0).astype(BF16)
        ends[c, h] = jnp.exp(g_end)
    inverse = {}
    for p in pairs:
        inverse[p] = jnp.where(row == col, 1.0, 0.0) - jnp.where(
            (row >> 1) == (col >> 1), couple[p], 0.0
        )
    level = 1
    while (2 << level) <= piece:
        keep = ((row >> (level + 1)) == (col >> (level + 1))) & ((row >> level) != (col >> level))
        left = {p: dot(inverse[p], jnp.where(keep, couple[p], 0.0)) for p in pairs}
        for p in pairs:
            inverse[p] = inverse[p] - dot(left[p], inverse[p])
        level += 1
    solved = {p: dot(inverse[p], solve[p]) for p in pairs}
    running = [None] * heads
    for c in range(count):
        slot = lax.rem(c - me + count, count)
        for h in range(heads):
            values, weighted = solved[c, h][:, :DV], solved[c, h][:, DV:]
            if c == 0:
                corrected = values
                out = None
            else:
                both = dot(
                    jnp.concatenate([weighted.astype(BF16), first[c, h]], axis=0), running[h]
                )
                corrected = values - both[:piece]
                out = both[piece:]
            both = dot(second[c, h], corrected)
            out = both[:piece] if out is None else out + both[:piece]
            running[h] = both[piece:] if c == 0 else ends[c, h] * running[h] + both[piece:]
            scale = lax.rsqrt(jnp.mean(out * out, axis=-1, keepdims=True) + EPS_NORM)
            attn[slot, :, h * DV : (h + 1) * DV] = (out * scale * gain[...]).astype(BF16)
    for h in range(heads):
        state[h] = running[h]


def delta(xs, smalls, where, taps, gain, heads, piece):
    count = len(xs)
    width = heads * (2 * DK + DV)
    return pl.pallas_call(
        functools.partial(delta_kernel, count, heads, piece),
        out_shape=(
            jax.ShapeDtypeStruct((count, piece, heads * DV), BF16),
            jax.ShapeDtypeStruct((heads, DK, DV), F32),
        ),
        in_specs=[VMEM] * (2 * count) + [SMEM, VMEM, VMEM],
        out_specs=(VMEM, VMEM),
        scratch_shapes=[
            pltpu.VMEM((8 + count * piece, width), F32),
            pltpu.VMEM((count, 8, piece), F32),
        ],
        compiler_params=pltpu.CompilerParams(vmem_limit_bytes=40 * MIB),
        cost_estimate=pl.CostEstimate(flops=int(4e9), bytes_accessed=4 * MIB, transcendentals=0),
        name="delta_rule",
    )(*xs, *smalls, where, taps, gain)


def project_kernel(count, cube, n_pieces, *refs):
    a_refs = refs[:count]
    where, gate, residual, gain = refs[count : count + 4]
    w_refs = refs[count + 4 : count + 4 + n_pieces]
    stream_out, normed_out, mixed, stream, weights, sems = refs[count + 4 + n_pieces :]
    me, req = where[0], where[1]
    depth = w_refs[0].shape[0]
    copies = []
    for j in range(n_pieces):
        copy = pltpu.make_async_copy(w_refs[j], weights.at[j], sems.at[j])
        copy.start()
        copies.append(copy)
    width = a_refs[0].shape[1]
    for k in range(count):
        cols = pl.ds(pl.multiple_of(lax.rem(me - k + count, count) * width, width), width)
        opened = silu(gate[:, cols].astype(F32))
        mixed[:, cols] = (a_refs[k][...].astype(F32) * opened).astype(BF16)
    total = residual[...].astype(F32)
    for j in range(n_pieces):
        copies[j].wait()
        block = (req ^ j) if cube else j
        lhs = mixed[:, pl.ds(pl.multiple_of(block * depth, depth), depth)]
        total += jnp.dot(lhs, weights[j], preferred_element_type=F32)
    rounded = total.astype(BF16)
    wide = rounded.astype(F32)
    scale = lax.rsqrt(jnp.mean(wide * wide, axis=-1, keepdims=True) + EPS_NORM)
    if not cube:
        stream_out[...] = rounded
        normed_out[...] = (wide * scale * gain[...]).astype(BF16)
        return
    stream[...] = rounded
    for j in range(n_pieces):
        cols = pl.ds(pl.multiple_of((req ^ j) * depth, depth), depth)
        part = stream[:, cols]
        stream_out[:, j * depth : (j + 1) * depth] = part
        normed_out[:, j * depth : (j + 1) * depth] = (
            part.astype(F32) * scale * gain[:, cols]
        ).astype(BF16)


def project(blocks, where, gate, residual, gain, pieces, cube):
    rows, width = residual.shape
    count, n_pieces = len(blocks), len(pieces)
    return pl.pallas_call(
        functools.partial(project_kernel, count, cube, n_pieces),
        out_shape=(jax.ShapeDtypeStruct((rows, width), BF16),) * 2,
        in_specs=[VMEM] * count + [SMEM, VMEM, VMEM, VMEM] + [ANY] * n_pieces,
        out_specs=(VMEM, VMEM),
        scratch_shapes=[
            pltpu.VMEM((rows, width), BF16),
            pltpu.VMEM((rows, width), BF16),
            pltpu.VMEM((n_pieces,) + pieces[0].shape, BF16),
            pltpu.SemaphoreType.DMA((n_pieces,)),
        ],
        compiler_params=pltpu.CompilerParams(vmem_limit_bytes=32 * MIB),
        cost_estimate=pl.CostEstimate(
            flops=2 * rows * width * width, bytes_accessed=8 * MIB, transcendentals=0
        ),
        name="output_projection",
    )(*blocks, where, gate, residual, gain, *pieces)


def parts_of(pieces):
    flat, place = [], []
    for j, piece in enumerate(pieces):
        for number, part in enumerate(piece):
            flat.append(part)
            place.append((j, number))
    return flat, place


def forward_kernel(count, places, axes, n_pieces, *refs):
    x_refs = refs[:count]
    refs = refs[count:]
    groups = []
    for place in places:
        groups.append(refs[: len(place)])
        refs = refs[len(place) :]
    outs = refs[:count]
    x, inner, *bufs = refs[count : count + 5]
    sems = refs[count + 5]
    rows = x_refs[0].shape[0]
    waits = []
    for g, (place, group, buf, axis) in enumerate(zip(places, groups, bufs, axes)):
        wait = [[] for _ in range(n_pieces)]
        for (j, number), ref in zip(place, group):
            size = ref.shape[axis]
            span = pl.ds(number * size, size)
            target = buf.at[j, span, :] if axis == 0 else buf.at[j, :, span]
            copy = pltpu.make_async_copy(ref, target, sems.at[g, 2 * j + number])
            wait[j].append(copy)
        waits.append(wait)
    for j in range(n_pieces):
        for wait in waits[:2]:
            for copy in wait[j]:
                copy.start()
    for j in range(n_pieces):
        for copy in waits[2][j]:
            copy.start()
    for k in range(count):
        x[k * rows : (k + 1) * rows, :] = x_refs[k][...]
    depth = bufs[0].shape[1]
    gate = up = None
    for j in range(n_pieces):
        for wait in waits[:2]:
            for copy in wait[j]:
                copy.wait()
        lhs = x[:, j * depth : (j + 1) * depth]
        gate_term = jnp.dot(lhs, bufs[0][j], preferred_element_type=F32)
        up_term = jnp.dot(lhs, bufs[1][j], preferred_element_type=F32)
        gate = gate_term if gate is None else gate + gate_term
        up = up_term if up is None else up + up_term
    inner[...] = (silu(gate) * up).astype(BF16)
    width = bufs[2].shape[2]
    for j in range(n_pieces):
        for copy in waits[2][j]:
            copy.wait()
        term = jnp.dot(inner[...], bufs[2][j], preferred_element_type=F32).astype(BF16)
        for k in range(count):
            outs[k][:, j * width : (j + 1) * width] = term[k * rows : (k + 1) * rows]


def forward(xs, gates, ups, downs):
    count, rows, width = len(xs), *xs[0].shape
    lists = [gates, ups, downs]
    axes = (0, 0, 1)
    flats, places = zip(*[parts_of(pieces) for pieces in lists])
    n_pieces = len(gates)
    bufs = []
    for pieces, axis in zip(lists, axes):
        shape = list(pieces[0][0].shape)
        shape[axis] = sum(part.shape[axis] for part in pieces[0])
        bufs.append(pltpu.VMEM((n_pieces, *shape), BF16))
    hidden = gates[0][0].shape[1]
    return pl.pallas_call(
        functools.partial(forward_kernel, count, places, axes, n_pieces),
        out_shape=(jax.ShapeDtypeStruct((rows, width), BF16),) * count,
        in_specs=[VMEM] * count + [ANY] * sum(len(flat) for flat in flats),
        out_specs=(VMEM,) * count,
        scratch_shapes=[
            pltpu.VMEM((count * rows, width), BF16),
            pltpu.VMEM((count * rows, hidden), BF16),
            *bufs,
            pltpu.SemaphoreType.DMA((3, 2 * n_pieces)),
        ],
        compiler_params=pltpu.CompilerParams(vmem_limit_bytes=48 * MIB),
        cost_estimate=pl.CostEstimate(
            flops=6 * count * rows * width * hidden, bytes_accessed=20 * MIB, transcendentals=0
        ),
        name="feed_forward",
    )(*xs, *[part for flat in flats for part in flat])


def finish_kernel(count, cube, n_blocks, *refs):
    y_refs = refs[:count]
    where, stream, out = refs[count:]
    rows, width = stream.shape
    req, alive = where[1], where[2]
    position = lax.broadcasted_iota(jnp.int32, (rows, 1), 0)
    size = width // n_blocks
    for j in range(n_blocks):
        span = slice(j * size, (j + 1) * size)
        total = stream[:, span].astype(F32)
        for y in y_refs:
            total += y[:, span].astype(F32)
        block = (req ^ j) if cube else j
        out[:, pl.ds(pl.multiple_of(block * size, size), size)] = jnp.where(
            position < alive, total, 0.0
        ).astype(BF16)


def finish(ys, where, stream, cube):
    count = len(ys)
    n_blocks = 8 if cube else 1
    return pl.pallas_call(
        functools.partial(finish_kernel, count, cube, n_blocks),
        out_shape=jax.ShapeDtypeStruct(stream.shape, BF16),
        in_specs=[VMEM] * count + [SMEM, VMEM],
        out_specs=VMEM,
        name="last_sum",
    )(*ys, where, stream)


def local(
    qkv_proj,
    gate_proj,
    residual,
    log_decay,
    beta_logit,
    lengths,
    slot_request,
    conv_weight,
    norm_gain,
    out_weight,
    mlp_gain,
    w_gate,
    w_up,
    w_down,
):
    me = lax.axis_index("seq")
    req = lax.axis_index("req")
    count = lax.axis_size("seq")
    cube = cubic()
    piece = qkv_proj.shape[1]
    channels = qkv_proj.shape[2]
    heads = HEADS // count
    ids = jnp.arange(slot_request.shape[0], dtype=jnp.int32)
    request = jnp.sum(jnp.where(ids == req, slot_request, 0))
    length = jnp.sum(jnp.where(ids == request, lengths, 0))
    alive = length - me * piece
    where = jnp.stack([me, req, alive]).astype(jnp.int32)
    local_position = jnp.arange(piece, dtype=jnp.int32)
    live = local_position < alive
    tokens = qkv_proj[0]

    beta = jax.nn.sigmoid(beta_logit[0].astype(F32)) * live[:, None]
    decay = jnp.where(live[:, None], log_decay[0], 0.0)
    targets = alive - (CONV - 1) + jnp.arange(CONV - 1, dtype=jnp.int32)
    select = (local_position[None, :] == targets[:, None]).astype(BF16)
    edge = jnp.dot(select, tokens, preferred_element_type=F32)
    block = channels // count
    edge_rows = (CONV - 1) * block // piece

    def share(target):
        start = target * heads
        parts = [
            lax.dynamic_slice_in_dim(tokens, start * DK, heads * DK, axis=1),
            lax.dynamic_slice_in_dim(tokens, HK + start * DK, heads * DK, axis=1),
            lax.dynamic_slice_in_dim(tokens, 2 * HK + start * DV, heads * DV, axis=1),
        ]
        strength = lax.dynamic_slice_in_dim(beta, start, heads, axis=1).T
        slope = lax.dynamic_slice_in_dim(decay, start, heads, axis=1).T
        pad = jnp.zeros((8 - 2 * heads, piece), F32)
        rim = lax.dynamic_slice_in_dim(edge, target * block, block, axis=1)
        small = jnp.concatenate([strength, slope, pad, rim.reshape(edge_rows, piece)], axis=0)
        return jnp.concatenate(parts, axis=1), small

    xs, smalls = [], []
    for k in range(count):
        big, small = share(lax.rem(me + k, count))
        if k:
            big, small = shift(big, "seq", count, k), shift(small, "seq", count, k)
        xs.append(big)
        smalls.append(small)
    conv_edge = sum(small[8:] for small in smalls).reshape(CONV - 1, block).astype(BF16)
    start = me * heads
    taps = jnp.concatenate(
        [
            lax.dynamic_slice_in_dim(conv_weight, start * DK, heads * DK, axis=1),
            lax.dynamic_slice_in_dim(conv_weight, HK + start * DK, heads * DK, axis=1),
            lax.dynamic_slice_in_dim(conv_weight, 2 * HK + start * DV, heads * DV, axis=1),
        ],
        axis=1,
    )
    attn, state = delta(xs, smalls, where, taps, norm_gain[None, :], heads, piece)

    if cube:
        rows = out_weight.shape[0]
        ring = [out_weight] + [shift(out_weight, "seq", count, k) for k in range(1, count)]
        line = jnp.zeros((count,) + out_weight.shape, BF16)
        for k, part in enumerate(ring):
            line = lax.dynamic_update_index_in_dim(line, part, lax.rem(me - k + count, count), 0)
        line = line.reshape(count * rows, -1)
        out_pieces = [
            parts[0] if len(parts) == 1 else jnp.concatenate(parts, axis=0)
            for parts in gather_req(line, 0)
        ]
        gates, ups, downs = gather_req(w_gate, 0), gather_req(w_up, 0), gather_req(w_down, 1)
    else:
        out_pieces = [lax.all_gather(out_weight, ("req", "seq"), axis=0, tiled=True)]
        gates, ups, downs = [gather_req(w_gate, 0)], [gather_req(w_up, 0)], [gather_req(w_down, 1)]

    blocks = [attn[0]] + [shift(attn[k], "seq", count, k) for k in range(1, count)]
    stream, normed = project(
        blocks, where, gate_proj[0], residual[0], mlp_gain[None, :], out_pieces, cube
    )
    tokens_in = [normed] + [shift(normed, "seq", count, k) for k in range(1, count)]
    ys = forward(tokens_in, gates, ups, downs)
    back = [ys[0]] + [shift(ys[k], "seq", count, count - k) for k in range(1, count)]
    hidden = finish(back, where, stream, cube)
    return hidden[None], state[None], conv_edge[None]


def solution(mesh):
    return jax.shard_map(
        local,
        mesh=mesh,
        in_specs=(
            P("req", "seq", None),
            P("req", "seq", None),
            P("req", "seq", None),
            P("req", "seq", None),
            P("req", "seq", None),
            P(),
            P(),
            P(),
            P(),
            P(("req", "seq"), None),
            P(),
            P("req", "seq"),
            P("req", "seq"),
            P("seq", "req"),
        ),
        out_specs=(P("req", "seq", None), P("req", "seq", None, None), P("req", None, "seq")),
        check_vma=False,
    )
```

```python
import functools

import jax
import jax.numpy as jnp
from jax import lax
from jax.experimental import pallas as pl
from jax.experimental.pallas import tpu as pltpu
from jax.sharding import PartitionSpec as P

HEADS = 8
DK = 128
DV = 256
CONV = 4
HK = HEADS * DK
EPS_NORM = 1e-05
EPS_UNIT = 1e-06
BF16 = jnp.bfloat16
F32 = jnp.float32
MIB = 1 << 20
STRIP = 256

VMEM = pl.BlockSpec(memory_space=pltpu.VMEM)
SMEM = pl.BlockSpec(memory_space=pltpu.SMEM)
ANY = pl.BlockSpec(memory_space=pl.ANY)


def dot(a, b):
    return jnp.dot(a.astype(BF16), b.astype(BF16), preferred_element_type=F32)


def dot_nt(a, b):
    return lax.dot_general(
        a.astype(BF16), b.astype(BF16), (((1,), (1,)), ((), ())), preferred_element_type=F32
    )


def silu(v):
    return v / (1.0 + jnp.exp(-v))


def shift(value, axis, count, steps):
    return lax.ppermute(value, axis, [(i, (i + steps) % count) for i in range(count)])


def flip(value, bits):
    return lax.ppermute(value, "req", [(i, i ^ bits) for i in range(lax.axis_size("req"))])


def cubic():
    return lax.axis_size("req") == 8


def along(value, count, pairs):
    return lax.ppermute(value, "seq", pairs)


def owners_of(count):
    me = lax.axis_index("seq")
    if count != 4:
        return jnp.stack([lax.rem(me - k + count, count) for k in range(count)]).astype(jnp.int32)
    low = me < 2
    return jnp.stack([me, me ^ 1, jnp.where(low, 2, 1), jnp.where(low, 3, 0)]).astype(jnp.int32)


def gather_line(value, count):
    if count != 4:
        return [[value]] + [[shift(value, "seq", count, k)] for k in range(1, count)]
    near = along(value, count, [(0, 1), (1, 0), (2, 3), (3, 2)])
    middle = along(value, count, [(1, 2), (2, 1)])
    far = along(value, count, [(0, 2), (3, 1)])
    middle_on = along(middle, count, [(1, 0), (2, 3)])
    far_on = along(far, count, [(1, 0), (2, 3)])
    return [[value], [near], [middle, middle_on], [far, far_on]]


def sum_line(parts, count):
    if count != 4:
        return [parts[0]] + [shift(parts[k], "seq", count, count - k) for k in range(1, count)]
    mine, near, middle, far = parts
    far_in = along(far, count, [(0, 1), (3, 2)])
    middle_in = along(middle, count, [(0, 1), (3, 2)])
    near = along(near, count, [(0, 1), (1, 0), (2, 3), (3, 2)])
    add = lambda u, v: (u.astype(F32) + v.astype(F32)).astype(BF16)
    far = along(add(far, far_in), count, [(2, 0), (1, 3)])
    middle = along(add(middle, middle_in), count, [(1, 2), (2, 1)])
    return [mine, near, middle, far]


def after(value, *earlier):
    return lax.optimization_barrier((value, *earlier))[0]


def gather_cube(block):
    mine = jnp.concatenate([block] + [flip(block, bits) for bits in (2, 4, 6)], axis=0)
    return [mine, flip(mine, 1)]


def length_of(where, lengths, slot_request):
    return lengths[slot_request[where[1]]]


def pack_kernel(count, heads, *refs):
    where, lengths, slot_request, tokens, gate, decay, logit = refs[:7]
    outs, (columns, edge, extra) = refs[7 : 7 + count], refs[7 + count :]
    me = where[0]
    piece, channels = tokens.shape
    block = channels // count
    heads_all = decay.shape[0]
    high = decay[...].astype(BF16)
    rest = decay[...] - high.astype(F32)
    middle = rest.astype(BF16)
    low = (rest - middle.astype(F32)).astype(BF16)
    for number, rows in enumerate((logit[...], high, middle, low)):
        columns[number * heads_all : (number + 1) * heads_all, :] = rows.astype(F32)
    first = length_of(where, lengths, slot_request) - (CONV - 1) - me * piece
    entry = lax.broadcasted_iota(jnp.int32, (8, piece), 0)
    spot = lax.broadcasted_iota(jnp.int32, (8, piece), 1)
    select = ((spot == first + entry) & (entry < CONV - 1)).astype(BF16)
    edge[...] = jnp.dot(select, tokens[...], preferred_element_type=F32)
    for k in range(count):
        target = lax.rem(me + k, count)
        start = target * heads

        def span(base, size):
            return pl.ds(pl.multiple_of(base + target * size, size), size)

        outs[k][:piece, : heads * DK] = tokens[:, span(0, heads * DK)]
        outs[k][:piece, heads * DK : 2 * heads * DK] = tokens[:, span(HK, heads * DK)]
        outs[k][:piece, 2 * heads * DK : block] = tokens[:, span(2 * HK, heads * DV)]
        outs[k][:piece, block:] = gate[:, span(0, heads * DV)]
        extra[...] = jnp.zeros(extra.shape, F32)
        for number in range(4):
            for h in range(heads):
                at = (number * heads + h) * piece
                extra[0:1, at : at + piece] = columns[pl.ds(number * heads_all + start + h, 1), :]
        extra[1:CONV, :] = edge[0 : CONV - 1, span(0, block)]
        outs[k][piece:, :block] = extra[...].astype(BF16)
        outs[k][piece:, block:] = jnp.zeros((16, heads * DV), BF16)


def pack(where, lengths, slot_request, tokens, gate, decay, logit, count):
    piece, channels = tokens.shape
    heads = HEADS // count
    block = channels // count
    return pl.pallas_call(
        functools.partial(pack_kernel, count, heads),
        out_shape=(jax.ShapeDtypeStruct((piece + 16, block + heads * DV), BF16),) * count,
        in_specs=[SMEM] * 3 + [VMEM] * 4,
        out_specs=(VMEM,) * count,
        scratch_shapes=[
            pltpu.VMEM((4 * HEADS, piece), F32),
            pltpu.VMEM((8, channels), F32),
            pltpu.VMEM((16, block), F32),
        ],
        name="pack",
    )(where, lengths, slot_request, tokens, gate, decay, logit)


def delta_kernel(count, heads, piece, *refs):
    x_refs, refs = refs[:count], refs[count:]
    where, lengths, slot_request, all_taps, gain, opened, state, xs, bs = refs
    me = where[0]
    length = length_of(where, lengths, slot_request)
    q0, k0, v0 = 0, heads * DK, 2 * heads * DK
    block = xs.shape[1]
    xs[pl.ds(0, 8), :] = jnp.zeros((8, block), F32)
    group = heads * piece
    lane = lax.broadcasted_iota(jnp.int32, (1, piece), 1)
    for k in range(count):
        c = lax.rem(me - k + count, count)
        at = pl.multiple_of(8 + c * piece, 8)
        xs[pl.ds(at, piece), :] = x_refs[k][:piece, :block].astype(F32)
        opened[c] = x_refs[k][:piece, block:]
        line = x_refs[k][piece:, :block].astype(F32)[0:1]
        strength = 1.0 / (1.0 + jnp.exp(-line[:, :group]))
        slope = line[:, group : 2 * group] + line[:, 2 * group : 3 * group] + line[:, 3 * group :]
        live = c * piece + lane < length
        for h in range(heads):
            span = slice(h * piece, (h + 1) * piece)
            bs[c, h : h + 1, :] = jnp.where(live, strength[:, span], 0.0)
            bs[c, heads + h : heads + h + 1, :] = jnp.where(live, slope[:, span], 0.0)
        bs[c, 2 * heads :, :] = jnp.zeros((8 - 2 * heads, piece), F32)

    def taps(i, col, width):
        base, step = (0, DK) if col < k0 else (HK, DK) if col < v0 else (2 * HK, DV)
        inside = col - (q0 if col < k0 else k0 if col < v0 else v0)
        at = pl.multiple_of(base + me * heads * step + inside, DK)
        return all_taps[i : i + 1, pl.ds(at, width)]

    def activated(c, col, width):
        total = None
        for i in range(CONV):
            rows = xs[pl.ds(8 - (CONV - 1) + i + c * piece, piece), pl.ds(col, width)]
            term = taps(i, col, width) * rows
            total = term if total is None else total + term
        return silu(total)

    def unit(v):
        return v * lax.rsqrt(jnp.sum(v * v, axis=-1, keepdims=True) + EPS_UNIT)

    row = lax.broadcasted_iota(jnp.int32, (piece, piece), 0)
    col = lax.broadcasted_iota(jnp.int32, (piece, piece), 1)
    upper = (row <= col).astype(F32)
    pairs = [(c, h) for c in range(count) for h in range(heads)]
    tabs = {}
    for c in range(count):
        rows = bs[c]
        cum = jnp.dot(rows, upper, precision=lax.Precision.HIGHEST, preferred_element_type=F32)
        wide = jnp.concatenate([cum, rows, jnp.zeros((piece - 16, piece), F32)], axis=0)
        tall = wide.T
        for h in range(heads):
            g_row = cum[heads + h : heads + h + 1, :]
            g_col = tall[:, heads + h : heads + h + 1]
            b_col = tall[:, 8 + h : 9 + h]
            tabs[c, h] = (g_row, g_col, b_col)
    couple, solve, first, second, ends = {}, {}, {}, {}, {}
    for c, h in pairs:
        g_row, g_col, b_col = tabs[c, h]
        q = unit(activated(c, q0 + h * DK, DK)) * DK ** (-0.5)
        k = unit(activated(c, k0 + h * DK, DK))
        v = activated(c, v0 + h * DV, DV)
        inner = dot_nt(jnp.concatenate([k, q], axis=0), k)
        spread = jnp.exp(jnp.where(row >= col, g_col - g_row, -1e30))
        couple[c, h] = jnp.where(row > col, inner[:piece] * spread * b_col, 0.0)
        grown = jnp.exp(g_col)
        g_end = g_row[:, piece - 1 : piece]
        to_end = jnp.exp(g_end - g_col) * k
        solve[c, h] = jnp.concatenate([b_col * v, (b_col * grown) * k], axis=1).astype(BF16)
        first[c, h] = (grown * q).astype(BF16)
        second[c, h] = jnp.concatenate([inner[piece:] * spread, to_end.T], axis=0).astype(BF16)
        ends[c, h] = jnp.exp(g_end)
    inverse = {}
    for p in pairs:
        inverse[p] = jnp.where(row == col, 1.0, 0.0) - jnp.where(
            (row >> 1) == (col >> 1), couple[p], 0.0
        )
    level = 1
    while (2 << level) <= piece:
        keep = ((row >> (level + 1)) == (col >> (level + 1))) & ((row >> level) != (col >> level))
        left = {p: dot(inverse[p], jnp.where(keep, couple[p], 0.0)) for p in pairs}
        for p in pairs:
            inverse[p] = inverse[p] - dot(left[p], inverse[p])
        level += 1
    solved = {p: dot(inverse[p], solve[p]) for p in pairs}
    running = [None] * heads
    for c in range(count):
        for h in range(heads):
            values, weighted = solved[c, h][:, :DV], solved[c, h][:, DV:]
            if c == 0:
                corrected = values
                out = None
            else:
                both = dot(
                    jnp.concatenate([weighted.astype(BF16), first[c, h]], axis=0), running[h]
                )
                corrected = values - both[:piece]
                out = both[piece:]
            both = dot(second[c, h], corrected)
            out = both[:piece] if out is None else out + both[:piece]
            running[h] = both[piece:] if c == 0 else ends[c, h] * running[h] + both[piece:]
            scale = lax.rsqrt(jnp.mean(out * out, axis=-1, keepdims=True) + EPS_NORM)
            span = slice(h * DV, (h + 1) * DV)
            gate = silu(opened[c, :, span].astype(F32))
            opened[c, :, span] = (out * scale * gain[...] * gate).astype(BF16)
    for h in range(heads):
        state[h] = running[h]


def delta(xs, where, lengths, slot_request, taps, gain, heads):
    count = len(xs)
    piece = xs[0].shape[0] - 16
    block = heads * (2 * DK + DV)
    return pl.pallas_call(
        functools.partial(delta_kernel, count, heads, piece),
        out_shape=(
            jax.ShapeDtypeStruct((count, piece, heads * DV), BF16),
            jax.ShapeDtypeStruct((heads, DK, DV), F32),
        ),
        in_specs=[VMEM] * count + [SMEM] * 3 + [VMEM] * 2,
        out_specs=(VMEM, VMEM),
        scratch_shapes=[
            pltpu.VMEM((8 + count * piece, block), F32),
            pltpu.VMEM((count, 8, piece), F32),
        ],
        compiler_params=pltpu.CompilerParams(vmem_limit_bytes=40 * MIB),
        cost_estimate=pl.CostEstimate(flops=int(4e9), bytes_accessed=4 * MIB, transcendentals=0),
        name="delta_rule",
    )(*xs, where, lengths, slot_request, taps, gain)


def project_kernel(count, orders, *refs):
    where, owners, mixed, refs = refs[0], refs[1], refs[2], refs[3:]
    parts, refs = refs[: len(orders)], refs[len(orders) :]
    outs, (weights, sems) = refs[:count], refs[count:]
    req = where[1]
    copies = []
    for j, (part, order) in enumerate(zip(parts, orders)):
        size = part.shape[0] // len(order or (0,))
        for i, bits in enumerate(order or (None,)):
            at = 0 if bits is None else pl.multiple_of((req ^ bits) * size, size)
            copies.append(
                pltpu.make_async_copy(
                    part.at[pl.ds(i * size, size), :], weights.at[pl.ds(at, size), :], sems.at[j, i]
                )
            )
            copies[-1].start()
    for copy in copies:
        copy.wait()
    for k in reversed(range(count)):
        outs[k][...] = jnp.dot(
            mixed[owners[k]], weights[...], preferred_element_type=F32
        ).astype(BF16)


def project(mixed, where, owners, parts):
    count, piece, depth = mixed.shape
    width = parts[0].shape[1]
    orders = [None] if len(parts) == 1 else [(0, 2, 4, 6), (1, 3, 5, 7)]
    return pl.pallas_call(
        functools.partial(project_kernel, count, orders),
        out_shape=(jax.ShapeDtypeStruct((piece, width), BF16),) * count,
        in_specs=[SMEM] * 2 + [VMEM] + [ANY] * len(parts),
        out_specs=(VMEM,) * count,
        scratch_shapes=[pltpu.VMEM((depth, width), BF16), pltpu.SemaphoreType.DMA((2, 4))],
        compiler_params=pltpu.CompilerParams(vmem_limit_bytes=24 * MIB),
        cost_estimate=pl.CostEstimate(
            flops=2 * count * piece * width * depth, bytes_accessed=4 * MIB, transcendentals=0
        ),
        name="output_projection",
    )(where, owners, mixed, *parts)


def norm_kernel(count, *refs):
    y_refs, (residual, gain, stream_out, normed_out) = refs[:count], refs[count:]
    total = y_refs[0][...].astype(F32)
    for y in y_refs[1:]:
        total += y[...].astype(F32)
    rounded = (residual[...].astype(F32) + total).astype(BF16)
    wide = rounded.astype(F32)
    scale = lax.rsqrt(jnp.mean(wide * wide, axis=-1, keepdims=True) + EPS_NORM)
    stream_out[...] = rounded
    normed_out[...] = (wide * scale * gain[...]).astype(BF16)


def norm(ys, residual, gain):
    count = len(ys)
    return pl.pallas_call(
        functools.partial(norm_kernel, count),
        out_shape=(jax.ShapeDtypeStruct(residual.shape, BF16),) * 2,
        in_specs=[VMEM] * (count + 2),
        out_specs=(VMEM, VMEM),
        name="stream_norm",
    )(*ys, residual, gain)


def unflatten(refs, counts):
    refs = iter(refs)
    return [[next(refs) for _ in range(count)] for count in counts]


def forward_kernel(terms, shares, strips, *refs):
    x_refs, weights, refs = refs[: sum(terms)], refs[sum(terms)], refs[sum(terms) + 1 :]
    count = len(terms)
    outs, (x, inner, spare, sems) = refs[:count], refs[count:]
    rows = x_refs[0].shape[0]
    depth = x.shape[1] // shares
    copies, spares = [], iter(range(sum(terms)))
    for k, arrays in enumerate(unflatten(x_refs, terms)):
        copies.append([])
        for i, array in enumerate(arrays):
            spot = next(spares)
            target = x.at[pl.ds(k * rows, rows), :] if i == 0 else spare.at[spot - k - 1]
            copy = pltpu.make_async_copy(array, target, sems.at[spot])
            copy.start()
            copies[k].append((copy, None if i == 0 else spot - k - 1))
    for k, group in enumerate(copies):
        for copy, spot in group:
            copy.wait()
            if spot is not None:
                x[k * rows : (k + 1) * rows, :] += spare[spot]

    def product(which, start, size):
        total = None
        for r in range(shares):
            low = (3 * r + which) * depth
            term = jnp.dot(
                x[:, r * depth : (r + 1) * depth],
                weights[low : low + depth, start : start + size],
                preferred_element_type=F32,
            )
            total = term if total is None else total + term
        return total

    for start, size in strips:
        opened, upward = product(0, start, size), product(1, start, size)
        inner[:, start : start + size] = (silu(opened) * upward).astype(BF16)
    for r in range(shares):
        low = (3 * r + 2) * depth
        term = dot_nt(inner[...], weights[low : low + depth, :]).astype(BF16)
        for k in range(count):
            outs[k][:, r * depth : (r + 1) * depth] = term[k * rows : (k + 1) * rows]


def forward(xs, weights, shares):
    rows, width = xs[0][0].shape
    count, hidden = len(xs), weights.shape[1]
    total = count * rows
    strips = [(start, min(STRIP, hidden - start)) for start in range(0, hidden, STRIP)]
    terms = [len(arrays) for arrays in xs]
    return pl.pallas_call(
        functools.partial(forward_kernel, terms, shares, strips),
        out_shape=(jax.ShapeDtypeStruct((rows, width), BF16),) * count,
        in_specs=[ANY] * sum(terms) + [VMEM],
        out_specs=(VMEM,) * count,
        scratch_shapes=[
            pltpu.VMEM((total, width), BF16),
            pltpu.VMEM((total, hidden), BF16),
            pltpu.VMEM((max(1, sum(terms) - count), rows, width), BF16),
            pltpu.SemaphoreType.DMA((sum(terms),)),
        ],
        compiler_params=pltpu.CompilerParams(vmem_limit_bytes=28 * MIB),
        cost_estimate=pl.CostEstimate(
            flops=6 * total * width * hidden, bytes_accessed=4 * MIB, transcendentals=0
        ),
        name="feed_forward",
    )(*sum(xs, []), weights)


def finish_kernel(count, *refs):
    y_refs, (where, lengths, slot_request, stream, out) = refs[:count], refs[count:]
    rows = stream.shape[0]
    position = where[0] * rows + lax.broadcasted_iota(jnp.int32, (rows, 1), 0)
    total = stream[...].astype(F32)
    for y in y_refs:
        total += y[...].astype(F32)
    live = position < length_of(where, lengths, slot_request)
    out[...] = jnp.where(live, total, 0.0).astype(BF16)


def finish(ys, where, lengths, slot_request, stream):
    count = len(ys)
    return pl.pallas_call(
        functools.partial(finish_kernel, count),
        out_shape=jax.ShapeDtypeStruct(stream.shape, BF16),
        in_specs=[VMEM] * count + [SMEM] * 3 + [VMEM],
        out_specs=VMEM,
        name="last_sum",
    )(*ys, where, lengths, slot_request, stream)


def local(
    qkv_proj,
    gate_proj,
    residual,
    log_decay,
    beta_logit,
    lengths,
    slot_request,
    conv_weight,
    norm_gain,
    out_weight,
    mlp_gain,
    w_gate,
    w_up,
    w_down,
):
    me = lax.axis_index("seq")
    req = lax.axis_index("req")
    count = lax.axis_size("seq")
    n_req = lax.axis_size("req")
    piece = qkv_proj.shape[1]
    heads = HEADS // count
    where = jnp.stack([me, req]).astype(jnp.int32)

    packed = pack(
        where, lengths, slot_request, qkv_proj[0], gate_proj[0], log_decay[0].T, beta_logit[0].T, count
    )
    xs = [packed[0]] + [shift(packed[k], "seq", count, k) for k in range(1, count)]
    block = qkv_proj.shape[2] // count
    conv_edge = sum(x[piece + 1 : piece + CONV, :block].astype(F32) for x in xs).astype(BF16)

    placed = lax.ppermute(
        out_weight,
        ("req", "seq"),
        [(i, (i % n_req) * count + i // n_req) for i in range(n_req * count)],
    )
    if cubic():
        out_parts = gather_cube(placed)
    else:
        out_parts = [lax.all_gather(placed, "req", axis=0, tiled=True)]
    weights = jnp.concatenate([w_gate, w_up, w_down.T], axis=0)
    weights = lax.all_gather(after(weights, out_parts[0], *xs[1:]), "req", axis=0, tiled=True)
    mixed, state = delta(xs, where, lengths, slot_request, conv_weight, norm_gain[None, :], heads)
    ys = project(mixed, where, owners_of(count), out_parts)
    stream, normed = norm(sum_line(ys, count), residual[0], mlp_gain[None, :])
    ys = forward(gather_line(normed, count), weights, n_req)
    hidden = finish(sum_line(ys, count), where, lengths, slot_request, stream)
    return hidden[None], state[None], conv_edge[None]


def solution(mesh):
    return jax.shard_map(
        local,
        mesh=mesh,
        in_specs=(
            P("req", "seq", None),
            P("req", "seq", None),
            P("req", "seq", None),
            P("req", "seq", None),
            P("req", "seq", None),
            P(),
            P(),
            P(),
            P(),
            P(("req", "seq"), None),
            P(),
            P("req", "seq"),
            P("req", "seq"),
            P("seq", "req"),
        ),
        out_specs=(P("req", "seq", None), P("req", "seq", None, None), P("req", None, "seq")),
        check_vma=False,
    )
```

```python
import functools

import jax
import jax.numpy as jnp
from jax import lax
from jax.experimental import pallas as pl
from jax.experimental.pallas import tpu as pltpu
from jax.sharding import PartitionSpec as P

HEADS = 8
DK = 128
DV = 256
CONV = 4
HK = HEADS * DK
EPS_NORM = 1e-05
EPS_UNIT = 1e-06
BF16 = jnp.bfloat16
F32 = jnp.float32
MIB = 1 << 20
STRIP = 256

VMEM = pl.BlockSpec(memory_space=pltpu.VMEM)
SMEM = pl.BlockSpec(memory_space=pltpu.SMEM)
ANY = pl.BlockSpec(memory_space=pl.ANY)


def dot(a, b):
    return jnp.dot(a.astype(BF16), b.astype(BF16), preferred_element_type=F32)


def dot_nt(a, b):
    return lax.dot_general(
        a.astype(BF16), b.astype(BF16), (((1,), (1,)), ((), ())), preferred_element_type=F32
    )


def silu(v):
    return v / (1.0 + jnp.exp(-v))


def shift(value, axis, count, steps):
    return lax.ppermute(value, axis, [(i, (i + steps) % count) for i in range(count)])


def flip(value, bits):
    return lax.ppermute(value, "req", [(i, i ^ bits) for i in range(lax.axis_size("req"))])


def cubic():
    return lax.axis_size("req") == 8


def along(value, count, pairs):
    return lax.ppermute(value, "seq", pairs)


def owners_of(count):
    me = lax.axis_index("seq")
    if count != 4:
        return jnp.stack([lax.rem(me - k + count, count) for k in range(count)]).astype(jnp.int32)
    low = me < 2
    return jnp.stack([me, me ^ 1, jnp.where(low, 2, 1), jnp.where(low, 3, 0)]).astype(jnp.int32)


def gather_line(value, count):
    if count != 4:
        return [[value]] + [[shift(value, "seq", count, k)] for k in range(1, count)]
    middle = along(value, count, [(1, 2), (2, 1)])
    far = along(value, count, [(0, 2), (3, 1)])
    middle_on = along(middle, count, [(1, 0), (2, 3)])
    far_on = along(far, count, [(1, 0), (2, 3)])
    near = along(value, count, [(0, 1), (1, 0), (2, 3), (3, 2)])
    return [[value], [near], [middle, middle_on], [far, far_on]]


def sum_line(parts, count):
    if count != 4:
        return [parts[0]] + [shift(parts[k], "seq", count, count - k) for k in range(1, count)]
    mine, near, middle, far = parts
    far_in = along(far, count, [(0, 1), (3, 2)])
    middle_in = along(middle, count, [(0, 1), (3, 2)])
    near = along(near, count, [(0, 1), (1, 0), (2, 3), (3, 2)])
    add = lambda u, v: (u.astype(F32) + v.astype(F32)).astype(BF16)
    far = along(add(far, far_in), count, [(2, 0), (1, 3)])
    middle = along(add(middle, middle_in), count, [(1, 2), (2, 1)])
    return [mine, near, middle, far]


def after(value, *earlier):
    return lax.optimization_barrier((value, *earlier))[0]


def gather_cube(block):
    mine = jnp.concatenate([block] + [flip(block, bits) for bits in (2, 4, 6)], axis=0)
    return [mine, flip(mine, 1)]


def length_of(where, lengths, slot_request):
    return lengths[slot_request[where[1]]]


def pack_kernel(count, heads, *refs):
    where, lengths, slot_request, tokens, gate, decay, logit = refs[:7]
    outs, (columns, edge, extra) = refs[7 : 7 + count], refs[7 + count :]
    me = where[0]
    piece, channels = tokens.shape
    block = channels // count
    heads_all = decay.shape[0]
    high = decay[...].astype(BF16)
    rest = decay[...] - high.astype(F32)
    middle = rest.astype(BF16)
    low = (rest - middle.astype(F32)).astype(BF16)
    for number, rows in enumerate((logit[...], high, middle, low)):
        columns[number * heads_all : (number + 1) * heads_all, :] = rows.astype(F32)
    first = length_of(where, lengths, slot_request) - (CONV - 1) - me * piece
    entry = lax.broadcasted_iota(jnp.int32, (8, piece), 0)
    spot = lax.broadcasted_iota(jnp.int32, (8, piece), 1)
    select = ((spot == first + entry) & (entry < CONV - 1)).astype(BF16)
    edge[...] = jnp.dot(select, tokens[...], preferred_element_type=F32)
    for k in range(count):
        target = lax.rem(me + k, count)
        start = target * heads

        def span(base, size):
            return pl.ds(pl.multiple_of(base + target * size, size), size)

        outs[k][:piece, : heads * DK] = tokens[:, span(0, heads * DK)]
        outs[k][:piece, heads * DK : 2 * heads * DK] = tokens[:, span(HK, heads * DK)]
        outs[k][:piece, 2 * heads * DK : block] = tokens[:, span(2 * HK, heads * DV)]
        outs[k][:piece, block:] = gate[:, span(0, heads * DV)]
        extra[...] = jnp.zeros(extra.shape, F32)
        for number in range(4):
            for h in range(heads):
                at = (number * heads + h) * piece
                extra[0:1, at : at + piece] = columns[pl.ds(number * heads_all + start + h, 1), :]
        extra[1:CONV, :] = edge[0 : CONV - 1, span(0, block)]
        outs[k][piece:, :block] = extra[...].astype(BF16)
        outs[k][piece:, block:] = jnp.zeros((16, heads * DV), BF16)


def pack(where, lengths, slot_request, tokens, gate, decay, logit, count):
    piece, channels = tokens.shape
    heads = HEADS // count
    block = channels // count
    return pl.pallas_call(
        functools.partial(pack_kernel, count, heads),
        out_shape=(jax.ShapeDtypeStruct((piece + 16, block + heads * DV), BF16),) * count,
        in_specs=[SMEM] * 3 + [VMEM] * 4,
        out_specs=(VMEM,) * count,
        scratch_shapes=[
            pltpu.VMEM((4 * HEADS, piece), F32),
            pltpu.VMEM((8, channels), F32),
            pltpu.VMEM((16, block), F32),
        ],
        name="pack",
    )(where, lengths, slot_request, tokens, gate, decay, logit)


def delta_kernel(count, heads, piece, *refs):
    x_refs, refs = refs[:count], refs[count:]
    where, lengths, slot_request, all_taps, gain, opened, state, xs, bs = refs
    me = where[0]
    length = length_of(where, lengths, slot_request)
    q0, k0, v0 = 0, heads * DK, 2 * heads * DK
    block = xs.shape[1]
    xs[pl.ds(0, 8), :] = jnp.zeros((8, block), F32)
    group = heads * piece
    lane = lax.broadcasted_iota(jnp.int32, (1, piece), 1)
    for k in range(count):
        c = lax.rem(me - k + count, count)
        at = pl.multiple_of(8 + c * piece, 8)
        xs[pl.ds(at, piece), :] = x_refs[k][:piece, :block].astype(F32)
        opened[c] = x_refs[k][:piece, block:]
        line = x_refs[k][piece:, :block].astype(F32)[0:1]
        strength = 1.0 / (1.0 + jnp.exp(-line[:, :group]))
        slope = line[:, group : 2 * group] + line[:, 2 * group : 3 * group] + line[:, 3 * group :]
        live = c * piece + lane < length
        for h in range(heads):
            span = slice(h * piece, (h + 1) * piece)
            bs[c, h : h + 1, :] = jnp.where(live, strength[:, span], 0.0)
            bs[c, heads + h : heads + h + 1, :] = jnp.where(live, slope[:, span], 0.0)
        bs[c, 2 * heads :, :] = jnp.zeros((8 - 2 * heads, piece), F32)

    def taps(i, col, width):
        base, step = (0, DK) if col < k0 else (HK, DK) if col < v0 else (2 * HK, DV)
        inside = col - (q0 if col < k0 else k0 if col < v0 else v0)
        at = pl.multiple_of(base + me * heads * step + inside, DK)
        return all_taps[i : i + 1, pl.ds(at, width)]

    def activated(c, col, width):
        total = None
        for i in range(CONV):
            rows = xs[pl.ds(8 - (CONV - 1) + i + c * piece, piece), pl.ds(col, width)]
            term = taps(i, col, width) * rows
            total = term if total is None else total + term
        return silu(total)

    def unit(v):
        return v * lax.rsqrt(jnp.sum(v * v, axis=-1, keepdims=True) + EPS_UNIT)

    row = lax.broadcasted_iota(jnp.int32, (piece, piece), 0)
    col = lax.broadcasted_iota(jnp.int32, (piece, piece), 1)
    upper = (row <= col).astype(F32)
    pairs = [(c, h) for c in range(count) for h in range(heads)]
    tabs = {}
    for c in range(count):
        rows = bs[c]
        cum = jnp.dot(rows, upper, precision=lax.Precision.HIGHEST, preferred_element_type=F32)
        wide = jnp.concatenate([cum, rows, jnp.zeros((piece - 16, piece), F32)], axis=0)
        tall = wide.T
        for h in range(heads):
            g_row = cum[heads + h : heads + h + 1, :]
            g_col = tall[:, heads + h : heads + h + 1]
            b_col = tall[:, 8 + h : 9 + h]
            tabs[c, h] = (g_row, g_col, b_col)
    couple, solve, first, second, ends = {}, {}, {}, {}, {}
    for c, h in pairs:
        g_row, g_col, b_col = tabs[c, h]
        q = unit(activated(c, q0 + h * DK, DK)) * DK ** (-0.5)
        k = unit(activated(c, k0 + h * DK, DK))
        v = activated(c, v0 + h * DV, DV)
        inner = dot_nt(jnp.concatenate([k, q], axis=0), k)
        spread = jnp.exp(jnp.where(row >= col, g_col - g_row, -1e30))
        couple[c, h] = jnp.where(row > col, inner[:piece] * spread * b_col, 0.0)
        grown = jnp.exp(g_col)
        g_end = g_row[:, piece - 1 : piece]
        to_end = jnp.exp(g_end - g_col) * k
        solve[c, h] = jnp.concatenate([b_col * v, (b_col * grown) * k], axis=1).astype(BF16)
        first[c, h] = (grown * q).astype(BF16)
        second[c, h] = jnp.concatenate([inner[piece:] * spread, to_end.T], axis=0).astype(BF16)
        ends[c, h] = jnp.exp(g_end)
    inverse = {}
    for p in pairs:
        inverse[p] = jnp.where(row == col, 1.0, 0.0) - jnp.where(
            (row >> 1) == (col >> 1), couple[p], 0.0
        )
    level = 1
    while (2 << level) <= piece:
        keep = ((row >> (level + 1)) == (col >> (level + 1))) & ((row >> level) != (col >> level))
        left = {p: dot(inverse[p], jnp.where(keep, couple[p], 0.0)) for p in pairs}
        for p in pairs:
            inverse[p] = inverse[p] - dot(left[p], inverse[p])
        level += 1
    solved = {p: dot(inverse[p], solve[p]) for p in pairs}
    running = [None] * heads
    for c in range(count):
        for h in range(heads):
            values, weighted = solved[c, h][:, :DV], solved[c, h][:, DV:]
            if c == 0:
                corrected = values
                out = None
            else:
                both = dot(
                    jnp.concatenate([weighted.astype(BF16), first[c, h]], axis=0), running[h]
                )
                corrected = values - both[:piece]
                out = both[piece:]
            both = dot(second[c, h], corrected)
            out = both[:piece] if out is None else out + both[:piece]
            running[h] = both[piece:] if c == 0 else ends[c, h] * running[h] + both[piece:]
            scale = lax.rsqrt(jnp.mean(out * out, axis=-1, keepdims=True) + EPS_NORM)
            span = slice(h * DV, (h + 1) * DV)
            gate = silu(opened[c, :, span].astype(F32))
            opened[c, :, span] = (out * scale * gain[...] * gate).astype(BF16)
    for h in range(heads):
        state[h] = running[h]


def delta(xs, where, lengths, slot_request, taps, gain, heads):
    count = len(xs)
    piece = xs[0].shape[0] - 16
    block = heads * (2 * DK + DV)
    return pl.pallas_call(
        functools.partial(delta_kernel, count, heads, piece),
        out_shape=(
            jax.ShapeDtypeStruct((count, piece, heads * DV), BF16),
            jax.ShapeDtypeStruct((heads, DK, DV), F32),
        ),
        in_specs=[VMEM] * count + [SMEM] * 3 + [VMEM] * 2,
        out_specs=(VMEM, VMEM),
        scratch_shapes=[
            pltpu.VMEM((8 + count * piece, block), F32),
            pltpu.VMEM((count, 8, piece), F32),
        ],
        compiler_params=pltpu.CompilerParams(vmem_limit_bytes=40 * MIB),
        cost_estimate=pl.CostEstimate(flops=int(4e9), bytes_accessed=4 * MIB, transcendentals=0),
        name="delta_rule",
    )(*xs, where, lengths, slot_request, taps, gain)


def project_kernel(count, orders, *refs):
    where, owners, mixed, refs = refs[0], refs[1], refs[2], refs[3:]
    parts, refs = refs[: len(orders)], refs[len(orders) :]
    outs, (weights, sems) = refs[:count], refs[count:]
    req = where[1]
    copies = []
    for j, (part, order) in enumerate(zip(parts, orders)):
        size = part.shape[0] // len(order or (0,))
        for i, bits in enumerate(order or (None,)):
            at = 0 if bits is None else pl.multiple_of((req ^ bits) * size, size)
            copies.append(
                pltpu.make_async_copy(
                    part.at[pl.ds(i * size, size), :], weights.at[pl.ds(at, size), :], sems.at[j, i]
                )
            )
            copies[-1].start()
    for copy in copies:
        copy.wait()
    for k in reversed(range(count)):
        outs[k][...] = jnp.dot(
            mixed[owners[k]], weights[...], preferred_element_type=F32
        ).astype(BF16)


def project(mixed, where, owners, parts):
    count, piece, depth = mixed.shape
    width = parts[0].shape[1]
    orders = [None] if len(parts) == 1 else [(0, 2, 4, 6), (1, 3, 5, 7)]
    return pl.pallas_call(
        functools.partial(project_kernel, count, orders),
        out_shape=(jax.ShapeDtypeStruct((piece, width), BF16),) * count,
        in_specs=[SMEM] * 2 + [VMEM] + [ANY] * len(parts),
        out_specs=(VMEM,) * count,
        scratch_shapes=[pltpu.VMEM((depth, width), BF16), pltpu.SemaphoreType.DMA((2, 4))],
        compiler_params=pltpu.CompilerParams(vmem_limit_bytes=24 * MIB),
        cost_estimate=pl.CostEstimate(
            flops=2 * count * piece * width * depth, bytes_accessed=4 * MIB, transcendentals=0
        ),
        name="output_projection",
    )(where, owners, mixed, *parts)


def norm_kernel(count, *refs):
    y_refs, (residual, gain, stream_out, normed_out) = refs[:count], refs[count:]
    total = y_refs[0][...].astype(F32)
    for y in y_refs[1:]:
        total += y[...].astype(F32)
    rounded = (residual[...].astype(F32) + total).astype(BF16)
    wide = rounded.astype(F32)
    scale = lax.rsqrt(jnp.mean(wide * wide, axis=-1, keepdims=True) + EPS_NORM)
    stream_out[...] = rounded
    normed_out[...] = (wide * scale * gain[...]).astype(BF16)


def norm(ys, residual, gain):
    count = len(ys)
    return pl.pallas_call(
        functools.partial(norm_kernel, count),
        out_shape=(jax.ShapeDtypeStruct(residual.shape, BF16),) * 2,
        in_specs=[VMEM] * (count + 2),
        out_specs=(VMEM, VMEM),
        name="stream_norm",
    )(*ys, residual, gain)


def unflatten(refs, counts):
    refs = iter(refs)
    return [[next(refs) for _ in range(count)] for count in counts]


def forward_kernel(terms, strips, *refs):
    x_refs, weights, refs = refs[: sum(terms)], refs[sum(terms)], refs[sum(terms) + 1 :]
    count = len(terms)
    outs, (x, inner, spare, gate_up, down, sems, weight_sems) = refs[:count], refs[count:]
    rows = x_refs[0].shape[0]
    shares, depth, hidden = down.shape
    copies, spares = [], iter(range(sum(terms)))
    for k, arrays in enumerate(unflatten(x_refs, terms)):
        copies.append([])
        for i, array in enumerate(arrays):
            spot = next(spares)
            target = x.at[pl.ds(k * rows, rows), :] if i == 0 else spare.at[spot - k - 1]
            copy = pltpu.make_async_copy(array, target, sems.at[spot])
            copy.start()
            copies[k].append((copy, None if i == 0 else spot - k - 1))
    weights = weights.reshape(shares, 3 * depth, hidden)
    weight_copies = []
    for i, strip in enumerate(strips):
        columns = pl.ds(*strip)
        weight_copies.append(
            pltpu.make_async_copy(
                weights.at[:, : 2 * depth, columns], gate_up.at[:, :, columns], weight_sems.at[i]
            )
        )
    weight_copies.append(
        pltpu.make_async_copy(weights.at[:, 2 * depth :, :], down, weight_sems.at[len(strips)])
    )
    for copy in weight_copies:
        copy.start()
    for k, group in enumerate(copies):
        for copy, spot in group:
            copy.wait()
            if spot is not None:
                x[k * rows : (k + 1) * rows, :] += spare[spot]

    def product(which, start, size):
        total = None
        for r in range(shares):
            term = jnp.dot(
                x[:, r * depth : (r + 1) * depth],
                gate_up[r, which * depth : (which + 1) * depth, start : start + size],
                preferred_element_type=F32,
            )
            total = term if total is None else total + term
        return total

    for (start, size), copy in zip(strips, weight_copies):
        copy.wait()
        opened, upward = product(0, start, size), product(1, start, size)
        inner[:, start : start + size] = (silu(opened) * upward).astype(BF16)
    weight_copies[-1].wait()
    for r in range(shares):
        term = dot_nt(inner[...], down[r]).astype(BF16)
        for k in range(count):
            outs[k][:, r * depth : (r + 1) * depth] = term[k * rows : (k + 1) * rows]


def forward(xs, weights, shares):
    rows, width = xs[0][0].shape
    count, hidden = len(xs), weights.shape[1]
    depth = width // shares
    total = count * rows
    strips = [(start, min(STRIP, hidden - start)) for start in range(0, hidden, STRIP)]
    terms = [len(arrays) for arrays in xs]
    return pl.pallas_call(
        functools.partial(forward_kernel, terms, strips),
        out_shape=(jax.ShapeDtypeStruct((rows, width), BF16),) * count,
        in_specs=[ANY] * (sum(terms) + 1),
        out_specs=(VMEM,) * count,
        scratch_shapes=[
            pltpu.VMEM((total, width), BF16),
            pltpu.VMEM((total, hidden), BF16),
            pltpu.VMEM((max(1, sum(terms) - count), rows, width), BF16),
            pltpu.VMEM((shares, 2 * depth, hidden), BF16),
            pltpu.VMEM((shares, depth, hidden), BF16),
            pltpu.SemaphoreType.DMA((sum(terms),)),
            pltpu.SemaphoreType.DMA((len(strips) + 1,)),
        ],
        compiler_params=pltpu.CompilerParams(vmem_limit_bytes=58 * MIB),
        cost_estimate=pl.CostEstimate(
            flops=6 * total * width * hidden, bytes_accessed=20 * MIB, transcendentals=0
        ),
        name="feed_forward",
    )(*sum(xs, []), weights)


def finish_kernel(count, *refs):
    y_refs, (where, lengths, slot_request, stream, out) = refs[:count], refs[count:]
    rows = stream.shape[0]
    position = where[0] * rows + lax.broadcasted_iota(jnp.int32, (rows, 1), 0)
    total = stream[...].astype(F32)
    for y in y_refs:
        total += y[...].astype(F32)
    live = position < length_of(where, lengths, slot_request)
    out[...] = jnp.where(live, total, 0.0).astype(BF16)


def finish(ys, where, lengths, slot_request, stream):
    count = len(ys)
    return pl.pallas_call(
        functools.partial(finish_kernel, count),
        out_shape=jax.ShapeDtypeStruct(stream.shape, BF16),
        in_specs=[VMEM] * count + [SMEM] * 3 + [VMEM],
        out_specs=VMEM,
        name="last_sum",
    )(*ys, where, lengths, slot_request, stream)


def local(
    qkv_proj,
    gate_proj,
    residual,
    log_decay,
    beta_logit,
    lengths,
    slot_request,
    conv_weight,
    norm_gain,
    out_weight,
    mlp_gain,
    w_gate,
    w_up,
    w_down,
):
    me = lax.axis_index("seq")
    req = lax.axis_index("req")
    count = lax.axis_size("seq")
    n_req = lax.axis_size("req")
    piece = qkv_proj.shape[1]
    heads = HEADS // count
    where = jnp.stack([me, req]).astype(jnp.int32)

    packed = pack(
        where, lengths, slot_request, qkv_proj[0], gate_proj[0], log_decay[0].T, beta_logit[0].T, count
    )
    xs = [packed[0]] + [shift(packed[k], "seq", count, k) for k in range(1, count)]
    block = qkv_proj.shape[2] // count
    conv_edge = sum(x[piece + 1 : piece + CONV, :block].astype(F32) for x in xs).astype(BF16)

    placed = lax.ppermute(
        out_weight,
        ("req", "seq"),
        [(i, (i % n_req) * count + i // n_req) for i in range(n_req * count)],
    )
    if cubic():
        out_parts = gather_cube(placed)
    else:
        out_parts = [lax.all_gather(placed, "req", axis=0, tiled=True)]
    weights = jnp.concatenate([w_gate, w_up, w_down.T], axis=0)
    weights = lax.all_gather(after(weights, out_parts[0], *xs[1:]), "req", axis=0, tiled=True)
    mixed, state = delta(xs, where, lengths, slot_request, conv_weight, norm_gain[None, :], heads)
    ys = project(mixed, where, owners_of(count), out_parts)
    stream, normed = norm(sum_line(ys, count), residual[0], mlp_gain[None, :])
    blocks = gather_line(normed, count)
    half = (count + 1) // 2
    ys = forward(blocks[:half], weights, n_req) + forward(blocks[half:], weights, n_req)
    hidden = finish(sum_line(ys, count), where, lengths, slot_request, stream)
    return hidden[None], state[None], conv_edge[None]


def solution(mesh):
    return jax.shard_map(
        local,
        mesh=mesh,
        in_specs=(
            P("req", "seq", None),
            P("req", "seq", None),
            P("req", "seq", None),
            P("req", "seq", None),
            P("req", "seq", None),
            P(),
            P(),
            P(),
            P(),
            P(("req", "seq"), None),
            P(),
            P("req", "seq"),
            P("req", "seq"),
            P("seq", "req"),
        ),
        out_specs=(P("req", "seq", None), P("req", "seq", None, None), P("req", None, "seq")),
        check_vma=False,
    )
```

```python
import functools

import jax
import jax.numpy as jnp
from jax import lax
from jax.experimental import pallas as pl
from jax.experimental.pallas import tpu as pltpu
from jax.sharding import PartitionSpec as P

HEADS = 8
DK = 128
DV = 256
CONV = 4
HK = HEADS * DK
EPS_NORM = 1e-05
EPS_UNIT = 1e-06
BF16 = jnp.bfloat16
F32 = jnp.float32
MIB = 1 << 20
STRIP = 256

VMEM = pl.BlockSpec(memory_space=pltpu.VMEM)
SMEM = pl.BlockSpec(memory_space=pltpu.SMEM)
ANY = pl.BlockSpec(memory_space=pl.ANY)


def dot(a, b):
    return jnp.dot(a.astype(BF16), b.astype(BF16), preferred_element_type=F32)


def dot_nt(a, b):
    return lax.dot_general(
        a.astype(BF16), b.astype(BF16), (((1,), (1,)), ((), ())), preferred_element_type=F32
    )


def silu(v):
    return v / (1.0 + jnp.exp(-v))


def shift(value, axis, count, steps):
    return lax.ppermute(value, axis, [(i, (i + steps) % count) for i in range(count)])


def flip(value, bits):
    return lax.ppermute(value, "req", [(i, i ^ bits) for i in range(lax.axis_size("req"))])


def cubic():
    return lax.axis_size("req") == 8


def along(value, count, pairs):
    return lax.ppermute(value, "seq", pairs)


def owners_of(count):
    me = lax.axis_index("seq")
    if count != 4:
        return jnp.stack([lax.rem(me - k + count, count) for k in range(count)]).astype(jnp.int32)
    low = me < 2
    return jnp.stack([me, me ^ 1, jnp.where(low, 2, 1), jnp.where(low, 3, 0)]).astype(jnp.int32)


def gather_line(value, count):
    if count != 4:
        return [[value]] + [[shift(value, "seq", count, k)] for k in range(1, count)]
    middle = along(value, count, [(1, 2), (2, 1)])
    far = along(value, count, [(0, 2), (3, 1)])
    middle_on = along(middle, count, [(1, 0), (2, 3)])
    far_on = along(far, count, [(1, 0), (2, 3)])
    near = along(value, count, [(0, 1), (1, 0), (2, 3), (3, 2)])
    return [[value], [near], [middle, middle_on], [far, far_on]]


def sum_line(parts, count):
    done = ()

    def part(k):
        return parts[k](done) if callable(parts[k]) else parts[k]

    if count != 4:
        return [part(0)] + [shift(part(k), "seq", count, count - k) for k in range(1, count)]

    def joined(k):
        mine = part(k)
        other = along(mine, count, [(0, 1), (3, 2)])
        return (mine.astype(F32) + other.astype(F32)).astype(BF16), mine

    far, done_far = joined(3)
    far_back = along(far, count, [(2, 0), (1, 3)])
    done = (done_far,)
    middle, done_middle = joined(2)
    done = (done_middle, far)
    near, mine = part(1), part(0)
    middle_back = along(after(middle, far_back, mine), count, [(1, 2), (2, 1)])
    near_back = along(near, count, [(0, 1), (1, 0), (2, 3), (3, 2)])
    return [mine, near_back, middle_back, far_back]


def after(value, *earlier):
    return lax.optimization_barrier((value, *earlier))[0]


def gather_cube(block):
    mine = jnp.concatenate([block] + [flip(block, bits) for bits in (2, 4, 6)], axis=0)
    return [mine, flip(mine, 1)]


def length_of(where, lengths, slot_request):
    return lengths[slot_request[where[1]]]


def pack_kernel(count, heads, *refs):
    where, lengths, slot_request, tokens, gate, decay, logit = refs[:7]
    outs, (columns, edge, extra) = refs[7 : 7 + count], refs[7 + count :]
    me = where[0]
    piece, channels = tokens.shape
    block = channels // count
    heads_all = decay.shape[0]
    high = decay[...].astype(BF16)
    rest = decay[...] - high.astype(F32)
    middle = rest.astype(BF16)
    low = (rest - middle.astype(F32)).astype(BF16)
    for number, rows in enumerate((logit[...], high, middle, low)):
        columns[number * heads_all : (number + 1) * heads_all, :] = rows.astype(F32)
    first = length_of(where, lengths, slot_request) - (CONV - 1) - me * piece
    entry = lax.broadcasted_iota(jnp.int32, (8, piece), 0)
    spot = lax.broadcasted_iota(jnp.int32, (8, piece), 1)
    select = ((spot == first + entry) & (entry < CONV - 1)).astype(BF16)
    edge[...] = jnp.dot(select, tokens[...], preferred_element_type=F32)
    for k in range(count):
        target = lax.rem(me + k, count)
        start = target * heads

        def span(base, size):
            return pl.ds(pl.multiple_of(base + target * size, size), size)

        outs[k][:piece, : heads * DK] = tokens[:, span(0, heads * DK)]
        outs[k][:piece, heads * DK : 2 * heads * DK] = tokens[:, span(HK, heads * DK)]
        outs[k][:piece, 2 * heads * DK : block] = tokens[:, span(2 * HK, heads * DV)]
        outs[k][:piece, block:] = gate[:, span(0, heads * DV)]
        extra[...] = jnp.zeros(extra.shape, F32)
        for number in range(4):
            for h in range(heads):
                at = (number * heads + h) * piece
                extra[0:1, at : at + piece] = columns[pl.ds(number * heads_all + start + h, 1), :]
        extra[1:CONV, :] = edge[0 : CONV - 1, span(0, block)]
        outs[k][piece:, :block] = extra[...].astype(BF16)
        outs[k][piece:, block:] = jnp.zeros((16, heads * DV), BF16)


def pack(where, lengths, slot_request, tokens, gate, decay, logit, count):
    piece, channels = tokens.shape
    heads = HEADS // count
    block = channels // count
    return pl.pallas_call(
        functools.partial(pack_kernel, count, heads),
        out_shape=(jax.ShapeDtypeStruct((piece + 16, block + heads * DV), BF16),) * count,
        in_specs=[SMEM] * 3 + [VMEM] * 4,
        out_specs=(VMEM,) * count,
        scratch_shapes=[
            pltpu.VMEM((4 * HEADS, piece), F32),
            pltpu.VMEM((8, channels), F32),
            pltpu.VMEM((16, block), F32),
        ],
        name="pack",
    )(where, lengths, slot_request, tokens, gate, decay, logit)


def delta_kernel(count, heads, piece, *refs):
    x_refs, refs = refs[:count], refs[count:]
    where, lengths, slot_request, all_taps, gain, opened, state, xs, bs = refs
    me = where[0]
    length = length_of(where, lengths, slot_request)
    q0, k0, v0 = 0, heads * DK, 2 * heads * DK
    block = xs.shape[1]
    xs[pl.ds(0, 8), :] = jnp.zeros((8, block), F32)
    group = heads * piece
    lane = lax.broadcasted_iota(jnp.int32, (1, piece), 1)
    for k in range(count):
        c = lax.rem(me - k + count, count)
        at = pl.multiple_of(8 + c * piece, 8)
        xs[pl.ds(at, piece), :] = x_refs[k][:piece, :block].astype(F32)
        opened[c] = x_refs[k][:piece, block:]
        line = x_refs[k][piece:, :block].astype(F32)[0:1]
        strength = 1.0 / (1.0 + jnp.exp(-line[:, :group]))
        slope = line[:, group : 2 * group] + line[:, 2 * group : 3 * group] + line[:, 3 * group :]
        live = c * piece + lane < length
        for h in range(heads):
            span = slice(h * piece, (h + 1) * piece)
            bs[c, h : h + 1, :] = jnp.where(live, strength[:, span], 0.0)
            bs[c, heads + h : heads + h + 1, :] = jnp.where(live, slope[:, span], 0.0)
        bs[c, 2 * heads :, :] = jnp.zeros((8 - 2 * heads, piece), F32)

    def taps(i, col, width):
        base, step = (0, DK) if col < k0 else (HK, DK) if col < v0 else (2 * HK, DV)
        inside = col - (q0 if col < k0 else k0 if col < v0 else v0)
        at = pl.multiple_of(base + me * heads * step + inside, DK)
        return all_taps[i : i + 1, pl.ds(at, width)]

    def activated(c, col, width):
        total = None
        for i in range(CONV):
            rows = xs[pl.ds(8 - (CONV - 1) + i + c * piece, piece), pl.ds(col, width)]
            term = taps(i, col, width) * rows
            total = term if total is None else total + term
        return silu(total)

    def unit(v):
        return v * lax.rsqrt(jnp.sum(v * v, axis=-1, keepdims=True) + EPS_UNIT)

    row = lax.broadcasted_iota(jnp.int32, (piece, piece), 0)
    col = lax.broadcasted_iota(jnp.int32, (piece, piece), 1)
    upper = (row <= col).astype(F32)
    pairs = [(c, h) for c in range(count) for h in range(heads)]
    tabs = {}
    for c in range(count):
        rows = bs[c]
        cum = jnp.dot(rows, upper, precision=lax.Precision.HIGHEST, preferred_element_type=F32)
        wide = jnp.concatenate([cum, rows, jnp.zeros((piece - 16, piece), F32)], axis=0)
        tall = wide.T
        for h in range(heads):
            g_row = cum[heads + h : heads + h + 1, :]
            g_col = tall[:, heads + h : heads + h + 1]
            b_col = tall[:, 8 + h : 9 + h]
            tabs[c, h] = (g_row, g_col, b_col)
    couple, solve, first, second, ends = {}, {}, {}, {}, {}
    for c, h in pairs:
        g_row, g_col, b_col = tabs[c, h]
        q = unit(activated(c, q0 + h * DK, DK)) * DK ** (-0.5)
        k = unit(activated(c, k0 + h * DK, DK))
        v = activated(c, v0 + h * DV, DV)
        inner = dot_nt(jnp.concatenate([k, q], axis=0), k)
        spread = jnp.exp(jnp.where(row >= col, g_col - g_row, -1e30))
        couple[c, h] = jnp.where(row > col, inner[:piece] * spread * b_col, 0.0)
        grown = jnp.exp(g_col)
        g_end = g_row[:, piece - 1 : piece]
        to_end = jnp.exp(g_end - g_col) * k
        solve[c, h] = jnp.concatenate([b_col * v, (b_col * grown) * k], axis=1).astype(BF16)
        first[c, h] = (grown * q).astype(BF16)
        second[c, h] = jnp.concatenate([inner[piece:] * spread, to_end.T], axis=0).astype(BF16)
        ends[c, h] = jnp.exp(g_end)
    inverse = {}
    for p in pairs:
        inverse[p] = jnp.where(row == col, 1.0, 0.0) - jnp.where(
            (row >> 1) == (col >> 1), couple[p], 0.0
        )
    level = 1
    while (2 << level) <= piece:
        keep = ((row >> (level + 1)) == (col >> (level + 1))) & ((row >> level) != (col >> level))
        left = {p: dot(inverse[p], jnp.where(keep, couple[p], 0.0)) for p in pairs}
        for p in pairs:
            inverse[p] = inverse[p] - dot(left[p], inverse[p])
        level += 1
    solved = {p: dot(inverse[p], solve[p]) for p in pairs}
    running = [None] * heads
    for c in range(count):
        for h in range(heads):
            values, weighted = solved[c, h][:, :DV], solved[c, h][:, DV:]
            if c == 0:
                corrected = values
                out = None
            else:
                both = dot(
                    jnp.concatenate([weighted.astype(BF16), first[c, h]], axis=0), running[h]
                )
                corrected = values - both[:piece]
                out = both[piece:]
            both = dot(second[c, h], corrected)
            out = both[:piece] if out is None else out + both[:piece]
            running[h] = both[piece:] if c == 0 else ends[c, h] * running[h] + both[piece:]
            scale = lax.rsqrt(jnp.mean(out * out, axis=-1, keepdims=True) + EPS_NORM)
            span = slice(h * DV, (h + 1) * DV)
            gate = silu(opened[c, :, span].astype(F32))
            opened[c, :, span] = (out * scale * gain[...] * gate).astype(BF16)
    for h in range(heads):
        state[h] = running[h]


def delta(xs, where, lengths, slot_request, taps, gain, heads):
    count = len(xs)
    piece = xs[0].shape[0] - 16
    block = heads * (2 * DK + DV)
    return pl.pallas_call(
        functools.partial(delta_kernel, count, heads, piece),
        out_shape=(
            jax.ShapeDtypeStruct((count, piece, heads * DV), BF16),
            jax.ShapeDtypeStruct((heads, DK, DV), F32),
        ),
        in_specs=[VMEM] * count + [SMEM] * 3 + [VMEM] * 2,
        out_specs=(VMEM, VMEM),
        scratch_shapes=[
            pltpu.VMEM((8 + count * piece, block), F32),
            pltpu.VMEM((count, 8, piece), F32),
        ],
        compiler_params=pltpu.CompilerParams(vmem_limit_bytes=40 * MIB),
        cost_estimate=pl.CostEstimate(flops=int(4e9), bytes_accessed=4 * MIB, transcendentals=0),
        name="delta_rule",
    )(*xs, where, lengths, slot_request, taps, gain)


def project_kernel(count, orders, *refs):
    where, owners, mixed, refs = refs[0], refs[1], refs[2], refs[3:]
    parts, refs = refs[: len(orders)], refs[len(orders) :]
    outs, (weights, sems) = refs[:count], refs[count:]
    req = where[1]
    copies = []
    for j, (part, order) in enumerate(zip(parts, orders)):
        size = part.shape[0] // len(order or (0,))
        for i, bits in enumerate(order or (None,)):
            at = 0 if bits is None else pl.multiple_of((req ^ bits) * size, size)
            copies.append(
                pltpu.make_async_copy(
                    part.at[pl.ds(i * size, size), :], weights.at[pl.ds(at, size), :], sems.at[j, i]
                )
            )
            copies[-1].start()
    for copy in copies:
        copy.wait()
    for k in reversed(range(count)):
        outs[k][...] = jnp.dot(
            mixed[owners[k]], weights[...], preferred_element_type=F32
        ).astype(BF16)


def project(mixed, where, owners, parts):
    count, piece, depth = mixed.shape
    width = parts[0].shape[1]
    orders = [None] if len(parts) == 1 else [(0, 2, 4, 6), (1, 3, 5, 7)]
    return pl.pallas_call(
        functools.partial(project_kernel, count, orders),
        out_shape=(jax.ShapeDtypeStruct((piece, width), BF16),) * count,
        in_specs=[SMEM] * 2 + [VMEM] + [ANY] * len(parts),
        out_specs=(VMEM,) * count,
        scratch_shapes=[pltpu.VMEM((depth, width), BF16), pltpu.SemaphoreType.DMA((2, 4))],
        compiler_params=pltpu.CompilerParams(vmem_limit_bytes=24 * MIB),
        cost_estimate=pl.CostEstimate(
            flops=2 * count * piece * width * depth, bytes_accessed=4 * MIB, transcendentals=0
        ),
        name="output_projection",
    )(where, owners, mixed, *parts)


def norm_kernel(count, *refs):
    y_refs, (residual, gain, stream_out, normed_out) = refs[:count], refs[count:]
    total = y_refs[0][...].astype(F32)
    for y in y_refs[1:]:
        total += y[...].astype(F32)
    rounded = (residual[...].astype(F32) + total).astype(BF16)
    wide = rounded.astype(F32)
    scale = lax.rsqrt(jnp.mean(wide * wide, axis=-1, keepdims=True) + EPS_NORM)
    stream_out[...] = rounded
    normed_out[...] = (wide * scale * gain[...]).astype(BF16)


def norm(ys, residual, gain):
    count = len(ys)
    return pl.pallas_call(
        functools.partial(norm_kernel, count),
        out_shape=(jax.ShapeDtypeStruct(residual.shape, BF16),) * 2,
        in_specs=[VMEM] * (count + 2),
        out_specs=(VMEM, VMEM),
        name="stream_norm",
    )(*ys, residual, gain)


def unflatten(refs, counts):
    refs = iter(refs)
    return [[next(refs) for _ in range(count)] for count in counts]


def forward_kernel(terms, strips, *refs):
    x_refs, weights, refs = refs[: sum(terms)], refs[sum(terms)], refs[sum(terms) + 1 :]
    count = len(terms)
    outs, (x, inner, spare, gate_up, down, sems, weight_sems) = refs[:count], refs[count:]
    rows = x_refs[0].shape[0]
    shares, depth, hidden = down.shape
    copies, spares = [], iter(range(sum(terms)))
    for k, arrays in enumerate(unflatten(x_refs, terms)):
        copies.append([])
        for i, array in enumerate(arrays):
            spot = next(spares)
            target = x.at[pl.ds(k * rows, rows), :] if i == 0 else spare.at[spot - k - 1]
            copy = pltpu.make_async_copy(array, target, sems.at[spot])
            copy.start()
            copies[k].append((copy, None if i == 0 else spot - k - 1))
    weights = weights.reshape(shares, 3 * depth, hidden)
    weight_copies = []
    for i, strip in enumerate(strips):
        columns = pl.ds(*strip)
        weight_copies.append(
            pltpu.make_async_copy(
                weights.at[:, : 2 * depth, columns], gate_up.at[:, :, columns], weight_sems.at[i]
            )
        )
    weight_copies.append(
        pltpu.make_async_copy(weights.at[:, 2 * depth :, :], down, weight_sems.at[len(strips)])
    )
    for copy in weight_copies:
        copy.start()
    for k, group in enumerate(copies):
        for copy, spot in group:
            copy.wait()
            if spot is not None:
                x[k * rows : (k + 1) * rows, :] += spare[spot]

    def product(which, start, size):
        total = None
        for r in range(shares):
            term = jnp.dot(
                x[:, r * depth : (r + 1) * depth],
                gate_up[r, which * depth : (which + 1) * depth, start : start + size],
                preferred_element_type=F32,
            )
            total = term if total is None else total + term
        return total

    for (start, size), copy in zip(strips, weight_copies):
        copy.wait()
        opened, upward = product(0, start, size), product(1, start, size)
        inner[:, start : start + size] = (silu(opened) * upward).astype(BF16)
    weight_copies[-1].wait()
    for r in range(shares):
        term = dot_nt(inner[...], down[r]).astype(BF16)
        for k in range(count):
            outs[k][:, r * depth : (r + 1) * depth] = term[k * rows : (k + 1) * rows]


def forward(xs, weights, shares):
    rows, width = xs[0][0].shape
    count, hidden = len(xs), weights.shape[1]
    depth = width // shares
    total = count * rows
    strips = [(start, min(STRIP, hidden - start)) for start in range(0, hidden, STRIP)]
    terms = [len(arrays) for arrays in xs]
    return pl.pallas_call(
        functools.partial(forward_kernel, terms, strips),
        out_shape=(jax.ShapeDtypeStruct((rows, width), BF16),) * count,
        in_specs=[ANY] * (sum(terms) + 1),
        out_specs=(VMEM,) * count,
        scratch_shapes=[
            pltpu.VMEM((total, width), BF16),
            pltpu.VMEM((total, hidden), BF16),
            pltpu.VMEM((max(1, sum(terms) - count), rows, width), BF16),
            pltpu.VMEM((shares, 2 * depth, hidden), BF16),
            pltpu.VMEM((shares, depth, hidden), BF16),
            pltpu.SemaphoreType.DMA((sum(terms),)),
            pltpu.SemaphoreType.DMA((len(strips) + 1,)),
        ],
        compiler_params=pltpu.CompilerParams(vmem_limit_bytes=58 * MIB),
        cost_estimate=pl.CostEstimate(
            flops=6 * total * width * hidden, bytes_accessed=20 * MIB, transcendentals=0
        ),
        name="feed_forward",
    )(*sum(xs, []), weights)


def finish_kernel(count, *refs):
    y_refs, (where, lengths, slot_request, stream, out) = refs[:count], refs[count:]
    rows = stream.shape[0]
    position = where[0] * rows + lax.broadcasted_iota(jnp.int32, (rows, 1), 0)
    total = stream[...].astype(F32)
    for y in y_refs:
        total += y[...].astype(F32)
    live = position < length_of(where, lengths, slot_request)
    out[...] = jnp.where(live, total, 0.0).astype(BF16)


def finish(ys, where, lengths, slot_request, stream):
    count = len(ys)
    return pl.pallas_call(
        functools.partial(finish_kernel, count),
        out_shape=jax.ShapeDtypeStruct(stream.shape, BF16),
        in_specs=[VMEM] * count + [SMEM] * 3 + [VMEM],
        out_specs=VMEM,
        name="last_sum",
    )(*ys, where, lengths, slot_request, stream)


def local(
    qkv_proj,
    gate_proj,
    residual,
    log_decay,
    beta_logit,
    lengths,
    slot_request,
    conv_weight,
    norm_gain,
    out_weight,
    mlp_gain,
    w_gate,
    w_up,
    w_down,
):
    me = lax.axis_index("seq")
    req = lax.axis_index("req")
    count = lax.axis_size("seq")
    n_req = lax.axis_size("req")
    piece = qkv_proj.shape[1]
    heads = HEADS // count
    where = jnp.stack([me, req]).astype(jnp.int32)

    packed = pack(
        where, lengths, slot_request, qkv_proj[0], gate_proj[0], log_decay[0].T, beta_logit[0].T, count
    )
    xs = [packed[0]] + [shift(packed[k], "seq", count, k) for k in range(1, count)]
    block = qkv_proj.shape[2] // count
    conv_edge = sum(x[piece + 1 : piece + CONV, :block].astype(F32) for x in xs).astype(BF16)

    placed = lax.ppermute(
        out_weight,
        ("req", "seq"),
        [(i, (i % n_req) * count + i // n_req) for i in range(n_req * count)],
    )
    if cubic():
        out_parts = gather_cube(placed)
    else:
        out_parts = [lax.all_gather(placed, "req", axis=0, tiled=True)]
    weights = jnp.concatenate([w_gate, w_up, w_down.T], axis=0)
    weights = lax.all_gather(after(weights, out_parts[0], *xs[1:]), "req", axis=0, tiled=True)
    mixed, state = delta(xs, where, lengths, slot_request, conv_weight, norm_gain[None, :], heads)
    ys = project(mixed, where, owners_of(count), out_parts)
    stream, normed = norm(sum_line(ys, count), residual[0], mlp_gain[None, :])
    blocks = gather_line(normed, count)
    first = min(2, count)
    nearest = []

    def near(k, done):
        if not nearest:
            nearest.extend(forward(after(blocks[:first], *done), weights, n_req))
        return nearest[k]

    def far(k, done):
        return forward(after([blocks[k]], *done, *blocks[first - 1]), weights, n_req)[0]

    parts = [functools.partial(near if k < first else far, k) for k in range(count)]
    hidden = finish(sum_line(parts, count), where, lengths, slot_request, stream)
    return hidden[None], state[None], conv_edge[None]


def solution(mesh):
    return jax.shard_map(
        local,
        mesh=mesh,
        in_specs=(
            P("req", "seq", None),
            P("req", "seq", None),
            P("req", "seq", None),
            P("req", "seq", None),
            P("req", "seq", None),
            P(),
            P(),
            P(),
            P(),
            P(("req", "seq"), None),
            P(),
            P("req", "seq"),
            P("req", "seq"),
            P("seq", "req"),
        ),
        out_specs=(P("req", "seq", None), P("req", "seq", None, None), P("req", None, "seq")),
        check_vma=False,
    )
```

```python
import functools

import jax
import jax.numpy as jnp
from jax import lax
from jax.experimental import pallas as pl
from jax.experimental.pallas import tpu as pltpu
from jax.sharding import PartitionSpec as P

HEADS = 8
DK = 128
DV = 256
CONV = 4
HK = HEADS * DK
EPS_NORM = 1e-05
EPS_UNIT = 1e-06
BF16 = jnp.bfloat16
F32 = jnp.float32
MIB = 1 << 20
STRIP = 256

VMEM = pl.BlockSpec(memory_space=pltpu.VMEM)
SMEM = pl.BlockSpec(memory_space=pltpu.SMEM)
ANY = pl.BlockSpec(memory_space=pl.ANY)


def dot(a, b):
    return jnp.dot(a.astype(BF16), b.astype(BF16), preferred_element_type=F32)


def dot_nt(a, b):
    return lax.dot_general(
        a.astype(BF16), b.astype(BF16), (((1,), (1,)), ((), ())), preferred_element_type=F32
    )


def silu(v):
    return v / (1.0 + jnp.exp(-v))


def shift(value, axis, count, steps):
    return lax.ppermute(value, axis, [(i, (i + steps) % count) for i in range(count)])


def flip(value, bits):
    return lax.ppermute(value, "req", [(i, i ^ bits) for i in range(lax.axis_size("req"))])


def cubic():
    return lax.axis_size("req") == 8


def along(value, count, pairs):
    return lax.ppermute(value, "seq", pairs)


def owners_of(count):
    me = lax.axis_index("seq")
    if count != 4:
        return jnp.stack([lax.rem(me - k + count, count) for k in range(count)]).astype(jnp.int32)
    low = me < 2
    return jnp.stack([me, me ^ 1, jnp.where(low, 2, 1), jnp.where(low, 3, 0)]).astype(jnp.int32)


def gather_line(value, count, *earlier):
    if count != 4:
        return [[value]] + [[shift(value, "seq", count, k)] for k in range(1, count)]
    middle = along(value, count, [(1, 2), (2, 1)])
    far = along(value, count, [(0, 2), (3, 1)])
    middle_on = along(after(middle, *earlier), count, [(1, 0), (2, 3)])
    far_on = along(far, count, [(1, 0), (2, 3)])
    near = along(value, count, [(0, 1), (1, 0), (2, 3), (3, 2)])
    return [[value], [near], [middle, middle_on], [far, far_on]]


def sum_line(parts, count):
    done = ()

    def part(k):
        return parts[k](done) if callable(parts[k]) else parts[k]

    if count != 4:
        return [part(0)] + [shift(part(k), "seq", count, count - k) for k in range(1, count)]

    def joined(k):
        mine = part(k)
        other = along(mine, count, [(0, 1), (3, 2)])
        return (mine.astype(F32) + other.astype(F32)).astype(BF16), mine

    far, done_far = joined(3)
    done = (done_far,)
    middle, done_middle = joined(2)
    done = (done_middle,)
    near, mine = part(1), part(0)
    far_back = along(after(far, mine), count, [(2, 0), (1, 3)])
    middle_back = along(after(middle, mine), count, [(1, 2), (2, 1)])
    near_back = along(near, count, [(0, 1), (1, 0), (2, 3), (3, 2)])
    return [mine, near_back, middle_back, far_back]


def after(value, *earlier):
    return lax.optimization_barrier((value, *earlier))[0]


def gather_cube(block):
    mine = jnp.concatenate([block] + [flip(block, bits) for bits in (2, 4, 6)], axis=0)
    return [mine, flip(mine, 1)]


def length_of(where, lengths, slot_request):
    return lengths[slot_request[where[1]]]


def pack_kernel(count, heads, *refs):
    where, lengths, slot_request, tokens, gate, decay, logit = refs[:7]
    outs, (columns, edge, extra) = refs[7 : 7 + count], refs[7 + count :]
    me = where[0]
    piece, channels = tokens.shape
    block = channels // count
    heads_all = decay.shape[0]
    high = decay[...].astype(BF16)
    rest = decay[...] - high.astype(F32)
    middle = rest.astype(BF16)
    low = (rest - middle.astype(F32)).astype(BF16)
    for number, rows in enumerate((logit[...], high, middle, low)):
        columns[number * heads_all : (number + 1) * heads_all, :] = rows.astype(F32)
    first = length_of(where, lengths, slot_request) - (CONV - 1) - me * piece
    entry = lax.broadcasted_iota(jnp.int32, (8, piece), 0)
    spot = lax.broadcasted_iota(jnp.int32, (8, piece), 1)
    select = ((spot == first + entry) & (entry < CONV - 1)).astype(BF16)
    edge[...] = jnp.dot(select, tokens[...], preferred_element_type=F32)
    for k in range(count):
        target = lax.rem(me + k, count)
        start = target * heads

        def span(base, size):
            return pl.ds(pl.multiple_of(base + target * size, size), size)

        outs[k][:piece, : heads * DK] = tokens[:, span(0, heads * DK)]
        outs[k][:piece, heads * DK : 2 * heads * DK] = tokens[:, span(HK, heads * DK)]
        outs[k][:piece, 2 * heads * DK : block] = tokens[:, span(2 * HK, heads * DV)]
        outs[k][:piece, block:] = gate[:, span(0, heads * DV)]
        extra[...] = jnp.zeros(extra.shape, F32)
        for number in range(4):
            for h in range(heads):
                at = (number * heads + h) * piece
                extra[0:1, at : at + piece] = columns[pl.ds(number * heads_all + start + h, 1), :]
        extra[1:CONV, :] = edge[0 : CONV - 1, span(0, block)]
        outs[k][piece:, :block] = extra[...].astype(BF16)
        outs[k][piece:, block:] = jnp.zeros((16, heads * DV), BF16)


def pack(where, lengths, slot_request, tokens, gate, decay, logit, count):
    piece, channels = tokens.shape
    heads = HEADS // count
    block = channels // count
    return pl.pallas_call(
        functools.partial(pack_kernel, count, heads),
        out_shape=(jax.ShapeDtypeStruct((piece + 16, block + heads * DV), BF16),) * count,
        in_specs=[SMEM] * 3 + [VMEM] * 4,
        out_specs=(VMEM,) * count,
        scratch_shapes=[
            pltpu.VMEM((4 * HEADS, piece), F32),
            pltpu.VMEM((8, channels), F32),
            pltpu.VMEM((16, block), F32),
        ],
        name="pack",
    )(where, lengths, slot_request, tokens, gate, decay, logit)


def delta_kernel(count, heads, piece, *refs):
    x_refs, refs = refs[:count], refs[count:]
    where, lengths, slot_request, all_taps, gain, opened, state, xs, bs = refs
    me = where[0]
    length = length_of(where, lengths, slot_request)
    q0, k0, v0 = 0, heads * DK, 2 * heads * DK
    block = xs.shape[1]
    xs[pl.ds(0, 8), :] = jnp.zeros((8, block), F32)
    group = heads * piece
    lane = lax.broadcasted_iota(jnp.int32, (1, piece), 1)
    for k in range(count):
        c = lax.rem(me - k + count, count)
        at = pl.multiple_of(8 + c * piece, 8)
        xs[pl.ds(at, piece), :] = x_refs[k][:piece, :block].astype(F32)
        opened[c] = x_refs[k][:piece, block:]
        line = x_refs[k][piece:, :block].astype(F32)[0:1]
        strength = 1.0 / (1.0 + jnp.exp(-line[:, :group]))
        slope = line[:, group : 2 * group] + line[:, 2 * group : 3 * group] + line[:, 3 * group :]
        live = c * piece + lane < length
        for h in range(heads):
            span = slice(h * piece, (h + 1) * piece)
            bs[c, h : h + 1, :] = jnp.where(live, strength[:, span], 0.0)
            bs[c, heads + h : heads + h + 1, :] = jnp.where(live, slope[:, span], 0.0)
        bs[c, 2 * heads :, :] = jnp.zeros((8 - 2 * heads, piece), F32)

    def taps(i, col, width):
        base, step = (0, DK) if col < k0 else (HK, DK) if col < v0 else (2 * HK, DV)
        inside = col - (q0 if col < k0 else k0 if col < v0 else v0)
        at = pl.multiple_of(base + me * heads * step + inside, DK)
        return all_taps[i : i + 1, pl.ds(at, width)]

    def activated(c, col, width):
        total = None
        for i in range(CONV):
            rows = xs[pl.ds(8 - (CONV - 1) + i + c * piece, piece), pl.ds(col, width)]
            term = taps(i, col, width) * rows
            total = term if total is None else total + term
        return silu(total)

    def unit(v):
        return v * lax.rsqrt(jnp.sum(v * v, axis=-1, keepdims=True) + EPS_UNIT)

    row = lax.broadcasted_iota(jnp.int32, (piece, piece), 0)
    col = lax.broadcasted_iota(jnp.int32, (piece, piece), 1)
    upper = (row <= col).astype(F32)
    pairs = [(c, h) for c in range(count) for h in range(heads)]
    tabs = {}
    for c in range(count):
        rows = bs[c]
        cum = jnp.dot(rows, upper, precision=lax.Precision.HIGHEST, preferred_element_type=F32)
        wide = jnp.concatenate([cum, rows, jnp.zeros((piece - 16, piece), F32)], axis=0)
        tall = wide.T
        for h in range(heads):
            g_row = cum[heads + h : heads + h + 1, :]
            g_col = tall[:, heads + h : heads + h + 1]
            b_col = tall[:, 8 + h : 9 + h]
            tabs[c, h] = (g_row, g_col, b_col)
    couple, solve, first, second, ends = {}, {}, {}, {}, {}
    for c, h in pairs:
        g_row, g_col, b_col = tabs[c, h]
        q = unit(activated(c, q0 + h * DK, DK)) * DK ** (-0.5)
        k = unit(activated(c, k0 + h * DK, DK))
        v = activated(c, v0 + h * DV, DV)
        inner = dot_nt(jnp.concatenate([k, q], axis=0), k)
        spread = jnp.exp(jnp.where(row >= col, g_col - g_row, -1e30))
        couple[c, h] = jnp.where(row > col, inner[:piece] * spread * b_col, 0.0)
        grown = jnp.exp(g_col)
        g_end = g_row[:, piece - 1 : piece]
        to_end = jnp.exp(g_end - g_col) * k
        solve[c, h] = jnp.concatenate([b_col * v, (b_col * grown) * k], axis=1).astype(BF16)
        first[c, h] = (grown * q).astype(BF16)
        second[c, h] = jnp.concatenate([inner[piece:] * spread, to_end.T], axis=0).astype(BF16)
        ends[c, h] = jnp.exp(g_end)
    inverse = {}
    for p in pairs:
        inverse[p] = jnp.where(row == col, 1.0, 0.0) - jnp.where(
            (row >> 1) == (col >> 1), couple[p], 0.0
        )
    level = 1
    while (2 << level) <= piece:
        keep = ((row >> (level + 1)) == (col >> (level + 1))) & ((row >> level) != (col >> level))
        left = {p: dot(inverse[p], jnp.where(keep, couple[p], 0.0)) for p in pairs}
        for p in pairs:
            inverse[p] = inverse[p] - dot(left[p], inverse[p])
        level += 1
    solved = {p: dot(inverse[p], solve[p]) for p in pairs}
    running = [None] * heads
    for c in range(count):
        for h in range(heads):
            values, weighted = solved[c, h][:, :DV], solved[c, h][:, DV:]
            if c == 0:
                corrected = values
                out = None
            else:
                both = dot(
                    jnp.concatenate([weighted.astype(BF16), first[c, h]], axis=0), running[h]
                )
                corrected = values - both[:piece]
                out = both[piece:]
            both = dot(second[c, h], corrected)
            out = both[:piece] if out is None else out + both[:piece]
            running[h] = both[piece:] if c == 0 else ends[c, h] * running[h] + both[piece:]
            scale = lax.rsqrt(jnp.mean(out * out, axis=-1, keepdims=True) + EPS_NORM)
            span = slice(h * DV, (h + 1) * DV)
            gate = silu(opened[c, :, span].astype(F32))
            opened[c, :, span] = (out * scale * gain[...] * gate).astype(BF16)
    for h in range(heads):
        state[h] = running[h]


def delta(xs, where, lengths, slot_request, taps, gain, heads):
    count = len(xs)
    piece = xs[0].shape[0] - 16
    block = heads * (2 * DK + DV)
    return pl.pallas_call(
        functools.partial(delta_kernel, count, heads, piece),
        out_shape=(
            jax.ShapeDtypeStruct((count, piece, heads * DV), BF16),
            jax.ShapeDtypeStruct((heads, DK, DV), F32),
        ),
        in_specs=[VMEM] * count + [SMEM] * 3 + [VMEM] * 2,
        out_specs=(VMEM, VMEM),
        scratch_shapes=[
            pltpu.VMEM((8 + count * piece, block), F32),
            pltpu.VMEM((count, 8, piece), F32),
        ],
        compiler_params=pltpu.CompilerParams(vmem_limit_bytes=40 * MIB),
        cost_estimate=pl.CostEstimate(flops=int(4e9), bytes_accessed=4 * MIB, transcendentals=0),
        name="delta_rule",
    )(*xs, where, lengths, slot_request, taps, gain)


def project_kernel(count, orders, *refs):
    where, owners, mixed, refs = refs[0], refs[1], refs[2], refs[3:]
    parts, refs = refs[: len(orders)], refs[len(orders) :]
    outs, (weights, sems) = refs[:count], refs[count:]
    req = where[1]
    copies = []
    for j, (part, order) in enumerate(zip(parts, orders)):
        size = part.shape[0] // len(order or (0,))
        for i, bits in enumerate(order or (None,)):
            at = 0 if bits is None else pl.multiple_of((req ^ bits) * size, size)
            copies.append(
                pltpu.make_async_copy(
                    part.at[pl.ds(i * size, size), :], weights.at[pl.ds(at, size), :], sems.at[j, i]
                )
            )
            copies[-1].start()
    for copy in copies:
        copy.wait()
    for k in reversed(range(count)):
        outs[k][...] = jnp.dot(
            mixed[owners[k]], weights[...], preferred_element_type=F32
        ).astype(BF16)


def project(mixed, where, owners, parts):
    count, piece, depth = mixed.shape
    width = parts[0].shape[1]
    orders = [None] if len(parts) == 1 else [(0, 2, 4, 6), (1, 3, 5, 7)]
    return pl.pallas_call(
        functools.partial(project_kernel, count, orders),
        out_shape=(jax.ShapeDtypeStruct((piece, width), BF16),) * count,
        in_specs=[SMEM] * 2 + [VMEM] + [ANY] * len(parts),
        out_specs=(VMEM,) * count,
        scratch_shapes=[pltpu.VMEM((depth, width), BF16), pltpu.SemaphoreType.DMA((2, 4))],
        compiler_params=pltpu.CompilerParams(vmem_limit_bytes=24 * MIB),
        cost_estimate=pl.CostEstimate(
            flops=2 * count * piece * width * depth, bytes_accessed=4 * MIB, transcendentals=0
        ),
        name="output_projection",
    )(where, owners, mixed, *parts)


def norm_kernel(count, *refs):
    y_refs, (residual, gain, stream_out, normed_out) = refs[:count], refs[count:]
    total = y_refs[0][...].astype(F32)
    for y in y_refs[1:]:
        total += y[...].astype(F32)
    rounded = (residual[...].astype(F32) + total).astype(BF16)
    wide = rounded.astype(F32)
    scale = lax.rsqrt(jnp.mean(wide * wide, axis=-1, keepdims=True) + EPS_NORM)
    stream_out[...] = rounded
    normed_out[...] = (wide * scale * gain[...]).astype(BF16)


def norm(ys, residual, gain):
    count = len(ys)
    return pl.pallas_call(
        functools.partial(norm_kernel, count),
        out_shape=(jax.ShapeDtypeStruct(residual.shape, BF16),) * 2,
        in_specs=[VMEM] * (count + 2),
        out_specs=(VMEM, VMEM),
        name="stream_norm",
    )(*ys, residual, gain)


def unflatten(refs, counts):
    refs = iter(refs)
    return [[next(refs) for _ in range(count)] for count in counts]


def forward_kernel(terms, shares, strips, *refs):
    x_refs, refs = refs[: sum(terms)], refs[sum(terms) :]
    early, weights, refs = refs[0], refs[1], refs[2:]
    count = len(terms)
    outs, (x, inner, spare, sems) = refs[:count], refs[count:]
    rows = x_refs[0].shape[0]
    depth = x.shape[1] // shares
    copies, spares = [], iter(range(sum(terms)))
    for k, arrays in enumerate(unflatten(x_refs, terms)):
        copies.append([])
        for i, array in enumerate(arrays):
            spot = next(spares)
            target = x.at[pl.ds(k * rows, rows), :] if i == 0 else spare.at[spot - k - 1]
            copy = pltpu.make_async_copy(array, target, sems.at[spot])
            copy.start()
            copies[k].append((copy, None if i == 0 else spot - k - 1))
    for k, group in enumerate(copies):
        for copy, spot in group:
            copy.wait()
            if spot is not None:
                x[k * rows : (k + 1) * rows, :] += spare[spot]

    half = depth // 2

    def product(sources, start, size):
        total = None
        for r in range(shares):
            at = r * depth
            for source, low, height in sources:
                low = low + r * (half if source is early else 5 * half)
                term = jnp.dot(
                    x[:, at : at + height],
                    source[low : low + height, start : start + size],
                    preferred_element_type=F32,
                )
                total = term if total is None else total + term
                at += height
        return total

    gate_rows = [(weights, 0, depth)]
    up_rows = [(early, 0, half), (weights, depth, half)]
    for start, size in strips:
        opened, upward = product(gate_rows, start, size), product(up_rows, start, size)
        inner[:, start : start + size] = (silu(opened) * upward).astype(BF16)
    for r in range(shares):
        low = (5 * r + 3) * half
        term = dot_nt(inner[...], weights[low : low + depth, :]).astype(BF16)
        for k in range(count):
            outs[k][:, r * depth : (r + 1) * depth] = term[k * rows : (k + 1) * rows]


def forward(xs, early, weights, shares):
    rows, width = xs[0][0].shape
    count, hidden = len(xs), weights.shape[1]
    total = count * rows
    strips = [(start, min(STRIP, hidden - start)) for start in range(0, hidden, STRIP)]
    terms = [len(arrays) for arrays in xs]
    return pl.pallas_call(
        functools.partial(forward_kernel, terms, shares, strips),
        out_shape=(jax.ShapeDtypeStruct((rows, width), BF16),) * count,
        in_specs=[ANY] * sum(terms) + [VMEM] * 2,
        out_specs=(VMEM,) * count,
        scratch_shapes=[
            pltpu.VMEM((total, width), BF16),
            pltpu.VMEM((total, hidden), BF16),
            pltpu.VMEM((max(1, sum(terms) - count), rows, width), BF16),
            pltpu.SemaphoreType.DMA((sum(terms),)),
        ],
        compiler_params=pltpu.CompilerParams(vmem_limit_bytes=24 * MIB),
        cost_estimate=pl.CostEstimate(
            flops=6 * total * width * hidden, bytes_accessed=20 * MIB, transcendentals=0
        ),
        name="feed_forward",
    )(*sum(xs, []), early, weights)


def finish_kernel(count, *refs):
    y_refs, (where, lengths, slot_request, stream, out) = refs[:count], refs[count:]
    rows = stream.shape[0]
    position = where[0] * rows + lax.broadcasted_iota(jnp.int32, (rows, 1), 0)
    total = stream[...].astype(F32)
    for y in y_refs:
        total += y[...].astype(F32)
    live = position < length_of(where, lengths, slot_request)
    out[...] = jnp.where(live, total, 0.0).astype(BF16)


def finish(ys, where, lengths, slot_request, stream):
    count = len(ys)
    return pl.pallas_call(
        functools.partial(finish_kernel, count),
        out_shape=jax.ShapeDtypeStruct(stream.shape, BF16),
        in_specs=[VMEM] * count + [SMEM] * 3 + [VMEM],
        out_specs=VMEM,
        name="last_sum",
    )(*ys, where, lengths, slot_request, stream)


def local(
    qkv_proj,
    gate_proj,
    residual,
    log_decay,
    beta_logit,
    lengths,
    slot_request,
    conv_weight,
    norm_gain,
    out_weight,
    mlp_gain,
    w_gate,
    w_up,
    w_down,
):
    me = lax.axis_index("seq")
    req = lax.axis_index("req")
    count = lax.axis_size("seq")
    n_req = lax.axis_size("req")
    piece = qkv_proj.shape[1]
    heads = HEADS // count
    where = jnp.stack([me, req]).astype(jnp.int32)

    packed = pack(
        where, lengths, slot_request, qkv_proj[0], gate_proj[0], log_decay[0].T, beta_logit[0].T, count
    )
    xs = [packed[0]] + [shift(packed[k], "seq", count, k) for k in range(1, count)]
    block = qkv_proj.shape[2] // count
    conv_edge = sum(x[piece + 1 : piece + CONV, :block].astype(F32) for x in xs).astype(BF16)

    placed = lax.ppermute(
        out_weight,
        ("req", "seq"),
        [(i, (i % n_req) * count + i // n_req) for i in range(n_req * count)],
    )
    if cubic():
        out_parts = gather_cube(placed)
    else:
        out_parts = [lax.all_gather(placed, "req", axis=0, tiled=True)]
    half = w_up.shape[0] // 2
    early = lax.all_gather(w_up[:half], "req", axis=0, tiled=True)
    weights = jnp.concatenate([w_gate, w_up[half:], w_down.T], axis=0)
    weights = after(weights, early, out_parts[0], *xs[1:])
    weights = lax.all_gather(weights, "req", axis=0, tiled=True)
    mixed, state = delta(xs, where, lengths, slot_request, conv_weight, norm_gain[None, :], heads)
    ys = project(mixed, where, owners_of(count), out_parts)
    stream, normed = norm(sum_line(ys, count), residual[0], mlp_gain[None, :])
    blocks = gather_line(normed, count, weights)
    first = min(2, count)
    nearest = []

    def near(k, done):
        if not nearest:
            nearest.extend(forward(after(blocks[:first], *done), early, weights, n_req))
        return nearest[k]

    def far(k, done):
        return forward(after([blocks[k]], *done, *blocks[first - 1]), early, weights, n_req)[0]

    parts = [functools.partial(near if k < first else far, k) for k in range(count)]
    hidden = finish(sum_line(parts, count), where, lengths, slot_request, stream)
    return hidden[None], state[None], conv_edge[None]


def solution(mesh):
    return jax.shard_map(
        local,
        mesh=mesh,
        in_specs=(
            P("req", "seq", None),
            P("req", "seq", None),
            P("req", "seq", None),
            P("req", "seq", None),
            P("req", "seq", None),
            P(),
            P(),
            P(),
            P(),
            P(("req", "seq"), None),
            P(),
            P("req", "seq"),
            P("req", "seq"),
            P("seq", "req"),
        ),
        out_specs=(P("req", "seq", None), P("req", "seq", None, None), P("req", None, "seq")),
        check_vma=False,
    )
```

```python
import functools

import jax
import jax.numpy as jnp
from jax import lax
from jax.experimental import pallas as pl
from jax.experimental.pallas import tpu as pltpu
from jax.sharding import PartitionSpec as P

HEADS = 8
DK = 128
DV = 256
CONV = 4
HK = HEADS * DK
EPS_NORM = 1e-05
EPS_UNIT = 1e-06
BF16 = jnp.bfloat16
F32 = jnp.float32
MIB = 1 << 20
STRIP = 256

VMEM = pl.BlockSpec(memory_space=pltpu.VMEM)
SMEM = pl.BlockSpec(memory_space=pltpu.SMEM)
ANY = pl.BlockSpec(memory_space=pl.ANY)


def dot(a, b):
    return jnp.dot(a.astype(BF16), b.astype(BF16), preferred_element_type=F32)


def dot_nt(a, b):
    return lax.dot_general(
        a.astype(BF16), b.astype(BF16), (((1,), (1,)), ((), ())), preferred_element_type=F32
    )


def silu(v):
    return v / (1.0 + jnp.exp(-v))


def shift(value, axis, count, steps):
    return lax.ppermute(value, axis, [(i, (i + steps) % count) for i in range(count)])


def flip(value, bits):
    return lax.ppermute(value, "req", [(i, i ^ bits) for i in range(lax.axis_size("req"))])


def cubic():
    return lax.axis_size("req") == 8


def along(value, count, pairs):
    return lax.ppermute(value, "seq", pairs)


def owners_of(count):
    me = lax.axis_index("seq")
    if count != 4:
        return jnp.stack([lax.rem(me - k + count, count) for k in range(count)]).astype(jnp.int32)
    low = me < 2
    return jnp.stack([me, me ^ 1, jnp.where(low, 2, 1), jnp.where(low, 3, 0)]).astype(jnp.int32)


def gather_line(value, count, *earlier):
    if count != 4:
        return [[value]] + [[shift(value, "seq", count, k)] for k in range(1, count)]
    middle = along(value, count, [(1, 2), (2, 1)])
    far = along(value, count, [(0, 2), (3, 1)])
    middle_on = along(after(middle, *earlier), count, [(1, 0), (2, 3)])
    far_on = along(far, count, [(1, 0), (2, 3)])
    near = along(value, count, [(0, 1), (1, 0), (2, 3), (3, 2)])
    return [[value], [near], [middle, middle_on], [far, far_on]]


def sum_line(parts, count):
    done = ()

    def part(k):
        return parts[k](done) if callable(parts[k]) else parts[k]

    if count != 4:
        return [part(0)] + [shift(part(k), "seq", count, count - k) for k in range(1, count)]

    def joined(k):
        mine = part(k)
        other = along(mine, count, [(0, 1), (3, 2)])
        return (mine.astype(F32) + other.astype(F32)).astype(BF16), mine

    far, done_far = joined(3)
    done = (done_far,)
    middle, done_middle = joined(2)
    done = (done_middle,)
    near, mine = part(1), part(0)
    far_back = along(after(far, mine), count, [(2, 0), (1, 3)])
    middle_back = along(after(middle, mine), count, [(1, 2), (2, 1)])
    near_back = along(near, count, [(0, 1), (1, 0), (2, 3), (3, 2)])
    return [mine, near_back, middle_back, far_back]


def after(value, *earlier):
    return lax.optimization_barrier((value, *earlier))[0]


def gather_cube(block):
    mine = jnp.concatenate([block] + [flip(block, bits) for bits in (2, 4, 6)], axis=0)
    return [mine, flip(mine, 1)]


def length_of(where, lengths, slot_request):
    return lengths[slot_request[where[1]]]


def pack_kernel(count, heads, *refs):
    where, lengths, slot_request, tokens, gate, decay, logit = refs[:7]
    outs, (columns, edge, extra) = refs[7 : 7 + count], refs[7 + count :]
    me = where[0]
    piece, channels = tokens.shape
    block = channels // count
    heads_all = decay.shape[0]
    high = decay[...].astype(BF16)
    rest = decay[...] - high.astype(F32)
    middle = rest.astype(BF16)
    low = (rest - middle.astype(F32)).astype(BF16)
    for number, rows in enumerate((logit[...], high, middle, low)):
        columns[number * heads_all : (number + 1) * heads_all, :] = rows.astype(F32)
    first = length_of(where, lengths, slot_request) - (CONV - 1) - me * piece
    entry = lax.broadcasted_iota(jnp.int32, (8, piece), 0)
    spot = lax.broadcasted_iota(jnp.int32, (8, piece), 1)
    select = ((spot == first + entry) & (entry < CONV - 1)).astype(BF16)
    edge[...] = jnp.dot(select, tokens[...], preferred_element_type=F32)
    for k in range(count):
        target = lax.rem(me + k, count)
        start = target * heads

        def span(base, size):
            return pl.ds(pl.multiple_of(base + target * size, size), size)

        outs[k][:piece, : heads * DK] = tokens[:, span(0, heads * DK)]
        outs[k][:piece, heads * DK : 2 * heads * DK] = tokens[:, span(HK, heads * DK)]
        outs[k][:piece, 2 * heads * DK : block] = tokens[:, span(2 * HK, heads * DV)]
        outs[k][:piece, block:] = gate[:, span(0, heads * DV)]
        extra[...] = jnp.zeros(extra.shape, F32)
        for number in range(4):
            for h in range(heads):
                at = (number * heads + h) * piece
                extra[0:1, at : at + piece] = columns[pl.ds(number * heads_all + start + h, 1), :]
        extra[1:CONV, :] = edge[0 : CONV - 1, span(0, block)]
        outs[k][piece:, :block] = extra[...].astype(BF16)
        outs[k][piece:, block:] = jnp.zeros((16, heads * DV), BF16)


def pack(where, lengths, slot_request, tokens, gate, decay, logit, count):
    piece, channels = tokens.shape
    heads = HEADS // count
    block = channels // count
    return pl.pallas_call(
        functools.partial(pack_kernel, count, heads),
        out_shape=(jax.ShapeDtypeStruct((piece + 16, block + heads * DV), BF16),) * count,
        in_specs=[SMEM] * 3 + [VMEM] * 4,
        out_specs=(VMEM,) * count,
        scratch_shapes=[
            pltpu.VMEM((4 * HEADS, piece), F32),
            pltpu.VMEM((8, channels), F32),
            pltpu.VMEM((16, block), F32),
        ],
        name="pack",
    )(where, lengths, slot_request, tokens, gate, decay, logit)


def delta_kernel(count, heads, piece, *refs):
    x_refs, refs = refs[:count], refs[count:]
    where, lengths, slot_request, all_taps, gain, opened, state, xs, bs = refs
    me = where[0]
    length = length_of(where, lengths, slot_request)
    q0, k0, v0 = 0, heads * DK, 2 * heads * DK
    block = xs.shape[1]
    xs[pl.ds(0, 8), :] = jnp.zeros((8, block), F32)
    group = heads * piece
    lane = lax.broadcasted_iota(jnp.int32, (1, piece), 1)
    for k in range(count):
        c = lax.rem(me - k + count, count)
        at = pl.multiple_of(8 + c * piece, 8)
        xs[pl.ds(at, piece), :] = x_refs[k][:piece, :block].astype(F32)
        opened[c] = x_refs[k][:piece, block:]
        line = x_refs[k][piece:, :block].astype(F32)[0:1]
        strength = 1.0 / (1.0 + jnp.exp(-line[:, :group]))
        slope = line[:, group : 2 * group] + line[:, 2 * group : 3 * group] + line[:, 3 * group :]
        live = c * piece + lane < length
        for h in range(heads):
            span = slice(h * piece, (h + 1) * piece)
            bs[c, h : h + 1, :] = jnp.where(live, strength[:, span], 0.0)
            bs[c, heads + h : heads + h + 1, :] = jnp.where(live, slope[:, span], 0.0)
        bs[c, 2 * heads :, :] = jnp.zeros((8 - 2 * heads, piece), F32)

    def taps(i, col, width):
        base, step = (0, DK) if col < k0 else (HK, DK) if col < v0 else (2 * HK, DV)
        inside = col - (q0 if col < k0 else k0 if col < v0 else v0)
        at = pl.multiple_of(base + me * heads * step + inside, DK)
        return all_taps[i : i + 1, pl.ds(at, width)]

    def activated(c, col, width):
        total = None
        for i in range(CONV):
            rows = xs[pl.ds(8 - (CONV - 1) + i + c * piece, piece), pl.ds(col, width)]
            term = taps(i, col, width) * rows
            total = term if total is None else total + term
        return silu(total)

    def unit(v):
        return v * lax.rsqrt(jnp.sum(v * v, axis=-1, keepdims=True) + EPS_UNIT)

    row = lax.broadcasted_iota(jnp.int32, (piece, piece), 0)
    col = lax.broadcasted_iota(jnp.int32, (piece, piece), 1)
    upper = (row <= col).astype(F32)
    pairs = [(c, h) for c in range(count) for h in range(heads)]
    tabs = {}
    for c in range(count):
        rows = bs[c]
        cum = jnp.dot(rows, upper, precision=lax.Precision.HIGHEST, preferred_element_type=F32)
        wide = jnp.concatenate([cum, rows, jnp.zeros((piece - 16, piece), F32)], axis=0)
        tall = wide.T
        for h in range(heads):
            g_row = cum[heads + h : heads + h + 1, :]
            g_col = tall[:, heads + h : heads + h + 1]
            b_col = tall[:, 8 + h : 9 + h]
            tabs[c, h] = (g_row, g_col, b_col)
    couple, solve, first, second, ends = {}, {}, {}, {}, {}
    for c, h in pairs:
        g_row, g_col, b_col = tabs[c, h]
        q = unit(activated(c, q0 + h * DK, DK)) * DK ** (-0.5)
        k = unit(activated(c, k0 + h * DK, DK))
        v = activated(c, v0 + h * DV, DV)
        inner = dot_nt(jnp.concatenate([k, q], axis=0), k)
        spread = jnp.exp(jnp.where(row >= col, g_col - g_row, -1e30))
        couple[c, h] = jnp.where(row > col, inner[:piece] * spread * b_col, 0.0)
        grown = jnp.exp(g_col)
        g_end = g_row[:, piece - 1 : piece]
        to_end = jnp.exp(g_end - g_col) * k
        solve[c, h] = jnp.concatenate([b_col * v, (b_col * grown) * k], axis=1).astype(BF16)
        first[c, h] = (grown * q).astype(BF16)
        second[c, h] = jnp.concatenate([inner[piece:] * spread, to_end.T], axis=0).astype(BF16)
        ends[c, h] = jnp.exp(g_end)
    inverse = {}
    for p in pairs:
        inverse[p] = jnp.where(row == col, 1.0, 0.0) - jnp.where(
            (row >> 1) == (col >> 1), couple[p], 0.0
        )
    level = 1
    while (2 << level) <= piece:
        keep = ((row >> (level + 1)) == (col >> (level + 1))) & ((row >> level) != (col >> level))
        left = {p: dot(inverse[p], jnp.where(keep, couple[p], 0.0)) for p in pairs}
        for p in pairs:
            inverse[p] = inverse[p] - dot(left[p], inverse[p])
        level += 1
    solved = {p: dot(inverse[p], solve[p]) for p in pairs}
    running = [None] * heads
    for c in range(count):
        for h in range(heads):
            values, weighted = solved[c, h][:, :DV], solved[c, h][:, DV:]
            if c == 0:
                corrected = values
                out = None
            else:
                both = dot(
                    jnp.concatenate([weighted.astype(BF16), first[c, h]], axis=0), running[h]
                )
                corrected = values - both[:piece]
                out = both[piece:]
            both = dot(second[c, h], corrected)
            out = both[:piece] if out is None else out + both[:piece]
            running[h] = both[piece:] if c == 0 else ends[c, h] * running[h] + both[piece:]
            scale = lax.rsqrt(jnp.mean(out * out, axis=-1, keepdims=True) + EPS_NORM)
            span = slice(h * DV, (h + 1) * DV)
            gate = silu(opened[c, :, span].astype(F32))
            opened[c, :, span] = (out * scale * gain[...] * gate).astype(BF16)
    for h in range(heads):
        state[h] = running[h]


def delta(xs, where, lengths, slot_request, taps, gain, heads):
    count = len(xs)
    piece = xs[0].shape[0] - 16
    block = heads * (2 * DK + DV)
    return pl.pallas_call(
        functools.partial(delta_kernel, count, heads, piece),
        out_shape=(
            jax.ShapeDtypeStruct((count, piece, heads * DV), BF16),
            jax.ShapeDtypeStruct((heads, DK, DV), F32),
        ),
        in_specs=[VMEM] * count + [SMEM] * 3 + [VMEM] * 2,
        out_specs=(VMEM, VMEM),
        scratch_shapes=[
            pltpu.VMEM((8 + count * piece, block), F32),
            pltpu.VMEM((count, 8, piece), F32),
        ],
        compiler_params=pltpu.CompilerParams(vmem_limit_bytes=40 * MIB),
        cost_estimate=pl.CostEstimate(flops=int(4e9), bytes_accessed=4 * MIB, transcendentals=0),
        name="delta_rule",
    )(*xs, where, lengths, slot_request, taps, gain)


def project_kernel(count, orders, *refs):
    where, owners, mixed, refs = refs[0], refs[1], refs[2], refs[3:]
    parts, refs = refs[: len(orders)], refs[len(orders) :]
    outs, (weights, sems) = refs[:count], refs[count:]
    req = where[1]
    copies = []
    for j, (part, order) in enumerate(zip(parts, orders)):
        size = part.shape[0] // len(order or (0,))
        for i, bits in enumerate(order or (None,)):
            at = 0 if bits is None else pl.multiple_of((req ^ bits) * size, size)
            copies.append(
                pltpu.make_async_copy(
                    part.at[pl.ds(i * size, size), :], weights.at[pl.ds(at, size), :], sems.at[j, i]
                )
            )
            copies[-1].start()
    for copy in copies:
        copy.wait()
    for k in reversed(range(count)):
        outs[k][...] = jnp.dot(
            mixed[owners[k]], weights[...], preferred_element_type=F32
        ).astype(BF16)


def project(mixed, where, owners, parts):
    count, piece, depth = mixed.shape
    width = parts[0].shape[1]
    orders = [None] if len(parts) == 1 else [(0, 2, 4, 6), (1, 3, 5, 7)]
    return pl.pallas_call(
        functools.partial(project_kernel, count, orders),
        out_shape=(jax.ShapeDtypeStruct((piece, width), BF16),) * count,
        in_specs=[SMEM] * 2 + [VMEM] + [ANY] * len(parts),
        out_specs=(VMEM,) * count,
        scratch_shapes=[pltpu.VMEM((depth, width), BF16), pltpu.SemaphoreType.DMA((2, 4))],
        compiler_params=pltpu.CompilerParams(vmem_limit_bytes=24 * MIB),
        cost_estimate=pl.CostEstimate(
            flops=2 * count * piece * width * depth, bytes_accessed=4 * MIB, transcendentals=0
        ),
        name="output_projection",
    )(where, owners, mixed, *parts)


def norm_kernel(count, *refs):
    y_refs, (residual, gain, stream_out, normed_out) = refs[:count], refs[count:]
    total = y_refs[0][...].astype(F32)
    for y in y_refs[1:]:
        total += y[...].astype(F32)
    rounded = (residual[...].astype(F32) + total).astype(BF16)
    wide = rounded.astype(F32)
    scale = lax.rsqrt(jnp.mean(wide * wide, axis=-1, keepdims=True) + EPS_NORM)
    stream_out[...] = rounded
    normed_out[...] = (wide * scale * gain[...]).astype(BF16)


def norm(ys, residual, gain):
    count = len(ys)
    return pl.pallas_call(
        functools.partial(norm_kernel, count),
        out_shape=(jax.ShapeDtypeStruct(residual.shape, BF16),) * 2,
        in_specs=[VMEM] * (count + 2),
        out_specs=(VMEM, VMEM),
        name="stream_norm",
    )(*ys, residual, gain)


def unflatten(refs, counts):
    refs = iter(refs)
    return [[next(refs) for _ in range(count)] for count in counts]


def forward_kernel(terms, shares, strips, *refs):
    x_refs, refs = refs[: sum(terms)], refs[sum(terms) :]
    early, weights, refs = refs[0], refs[1], refs[2:]
    count = len(terms)
    outs, (x, inner, spare, sems) = refs[:count], refs[count:]
    rows = x_refs[0].shape[0]
    depth = x.shape[1] // shares
    copies, spares = [], iter(range(sum(terms)))
    for k, arrays in enumerate(unflatten(x_refs, terms)):
        copies.append([])
        for i, array in enumerate(arrays):
            spot = next(spares)
            target = x.at[pl.ds(k * rows, rows), :] if i == 0 else spare.at[spot - k - 1]
            copy = pltpu.make_async_copy(array, target, sems.at[spot])
            copy.start()
            copies[k].append((copy, None if i == 0 else spot - k - 1))
    for k, group in enumerate(copies):
        for copy, spot in group:
            copy.wait()
            if spot is not None:
                x[k * rows : (k + 1) * rows, :] += spare[spot]

    half = depth // 2

    def product(which, start, size):
        total = None
        for r in range(shares):
            columns, low = slice(start, start + size), 5 * r * half
            if which == 0:
                rhs = weights[low : low + depth, columns]
            else:
                ahead = early[r * half : (r + 1) * half, columns]
                rest = weights[low + depth : low + depth + half, columns]
                rhs = jnp.concatenate([ahead, rest], axis=0)
            term = jnp.dot(
                x[:, r * depth : (r + 1) * depth], rhs, preferred_element_type=F32
            )
            total = term if total is None else total + term
        return total

    for start, size in strips:
        opened, upward = product(0, start, size), product(1, start, size)
        inner[:, start : start + size] = (silu(opened) * upward).astype(BF16)
    for r in range(shares):
        low = (5 * r + 3) * half
        term = dot_nt(inner[...], weights[low : low + depth, :]).astype(BF16)
        for k in range(count):
            outs[k][:, r * depth : (r + 1) * depth] = term[k * rows : (k + 1) * rows]


def forward(xs, early, weights, shares):
    rows, width = xs[0][0].shape
    count, hidden = len(xs), weights.shape[1]
    total = count * rows
    strips = [(start, min(STRIP, hidden - start)) for start in range(0, hidden, STRIP)]
    terms = [len(arrays) for arrays in xs]
    return pl.pallas_call(
        functools.partial(forward_kernel, terms, shares, strips),
        out_shape=(jax.ShapeDtypeStruct((rows, width), BF16),) * count,
        in_specs=[ANY] * sum(terms) + [VMEM] * 2,
        out_specs=(VMEM,) * count,
        scratch_shapes=[
            pltpu.VMEM((total, width), BF16),
            pltpu.VMEM((total, hidden), BF16),
            pltpu.VMEM((max(1, sum(terms) - count), rows, width), BF16),
            pltpu.SemaphoreType.DMA((sum(terms),)),
        ],
        compiler_params=pltpu.CompilerParams(vmem_limit_bytes=24 * MIB),
        cost_estimate=pl.CostEstimate(
            flops=6 * total * width * hidden, bytes_accessed=20 * MIB, transcendentals=0
        ),
        name="feed_forward",
    )(*sum(xs, []), early, weights)


def finish_kernel(count, *refs):
    y_refs, (where, lengths, slot_request, stream, out) = refs[:count], refs[count:]
    rows = stream.shape[0]
    position = where[0] * rows + lax.broadcasted_iota(jnp.int32, (rows, 1), 0)
    total = stream[...].astype(F32)
    for y in y_refs:
        total += y[...].astype(F32)
    live = position < length_of(where, lengths, slot_request)
    out[...] = jnp.where(live, total, 0.0).astype(BF16)


def finish(ys, where, lengths, slot_request, stream):
    count = len(ys)
    return pl.pallas_call(
        functools.partial(finish_kernel, count),
        out_shape=jax.ShapeDtypeStruct(stream.shape, BF16),
        in_specs=[VMEM] * count + [SMEM] * 3 + [VMEM],
        out_specs=VMEM,
        name="last_sum",
    )(*ys, where, lengths, slot_request, stream)


def local(
    qkv_proj,
    gate_proj,
    residual,
    log_decay,
    beta_logit,
    lengths,
    slot_request,
    conv_weight,
    norm_gain,
    out_weight,
    mlp_gain,
    w_gate,
    w_up,
    w_down,
):
    me = lax.axis_index("seq")
    req = lax.axis_index("req")
    count = lax.axis_size("seq")
    n_req = lax.axis_size("req")
    piece = qkv_proj.shape[1]
    heads = HEADS // count
    where = jnp.stack([me, req]).astype(jnp.int32)

    packed = pack(
        where, lengths, slot_request, qkv_proj[0], gate_proj[0], log_decay[0].T, beta_logit[0].T, count
    )
    xs = [packed[0]] + [shift(packed[k], "seq", count, k) for k in range(1, count)]
    block = qkv_proj.shape[2] // count
    conv_edge = sum(x[piece + 1 : piece + CONV, :block].astype(F32) for x in xs).astype(BF16)

    placed = lax.ppermute(
        out_weight,
        ("req", "seq"),
        [(i, (i % n_req) * count + i // n_req) for i in range(n_req * count)],
    )
    if cubic():
        out_parts = gather_cube(placed)
    else:
        out_parts = [lax.all_gather(placed, "req", axis=0, tiled=True)]
    half = w_up.shape[0] // 2
    early = lax.all_gather(w_up[:half], "req", axis=0, tiled=True)
    weights = jnp.concatenate([w_gate, w_up[half:], w_down.T], axis=0)
    weights = after(weights, early, out_parts[0], *xs[1:])
    weights = lax.all_gather(weights, "req", axis=0, tiled=True)
    mixed, state = delta(xs, where, lengths, slot_request, conv_weight, norm_gain[None, :], heads)
    ys = project(mixed, where, owners_of(count), out_parts)
    stream, normed = norm(sum_line(ys, count), residual[0], mlp_gain[None, :])
    blocks = gather_line(normed, count, weights)
    first = min(2, count)
    nearest = []

    def near(k, done):
        if not nearest:
            nearest.extend(forward(after(blocks[:first], *done), early, weights, n_req))
        return nearest[k]

    def far(k, done):
        return forward(after([blocks[k]], *done, *blocks[first - 1]), early, weights, n_req)[0]

    parts = [functools.partial(near if k < first else far, k) for k in range(count)]
    hidden = finish(sum_line(parts, count), where, lengths, slot_request, stream)
    return hidden[None], state[None], conv_edge[None]


def solution(mesh):
    return jax.shard_map(
        local,
        mesh=mesh,
        in_specs=(
            P("req", "seq", None),
            P("req", "seq", None),
            P("req", "seq", None),
            P("req", "seq", None),
            P("req", "seq", None),
            P(),
            P(),
            P(),
            P(),
            P(("req", "seq"), None),
            P(),
            P("req", "seq"),
            P("req", "seq"),
            P("seq", "req"),
        ),
        out_specs=(P("req", "seq", None), P("req", "seq", None, None), P("req", None, "seq")),
        check_vma=False,
    )
```

```python
import functools

import jax
import jax.numpy as jnp
from jax import lax
from jax.experimental import pallas as pl
from jax.experimental.pallas import tpu as pltpu
from jax.sharding import PartitionSpec as P

HEADS = 8
DK = 128
DV = 256
CONV = 4
HK = HEADS * DK
EPS_NORM = 1e-05
EPS_UNIT = 1e-06
BF16 = jnp.bfloat16
F32 = jnp.float32
MIB = 1 << 20
STRIP = 256

VMEM = pl.BlockSpec(memory_space=pltpu.VMEM)
SMEM = pl.BlockSpec(memory_space=pltpu.SMEM)
ANY = pl.BlockSpec(memory_space=pl.ANY)


def dot(a, b):
    return jnp.dot(a.astype(BF16), b.astype(BF16), preferred_element_type=F32)


def dot_nt(a, b):
    return lax.dot_general(
        a.astype(BF16), b.astype(BF16), (((1,), (1,)), ((), ())), preferred_element_type=F32
    )


def silu(v):
    return v / (1.0 + jnp.exp(-v))


def shift(value, axis, count, steps):
    return lax.ppermute(value, axis, [(i, (i + steps) % count) for i in range(count)])


def flip(value, bits):
    return lax.ppermute(value, "req", [(i, i ^ bits) for i in range(lax.axis_size("req"))])


def cubic():
    return lax.axis_size("req") == 8


def along(value, count, pairs):
    return lax.ppermute(value, "seq", pairs)


def owners_of(count):
    me = lax.axis_index("seq")
    if count != 4:
        return jnp.stack([lax.rem(me - k + count, count) for k in range(count)]).astype(jnp.int32)
    low = me < 2
    return jnp.stack([me, me ^ 1, jnp.where(low, 2, 1), jnp.where(low, 3, 0)]).astype(jnp.int32)


def gather_line(value, count, *earlier):
    if count != 4:
        return [[value]] + [[shift(value, "seq", count, k)] for k in range(1, count)]
    middle = along(value, count, [(1, 2), (2, 1)])
    far = along(value, count, [(0, 2), (3, 1)])
    middle_on = along(after(middle, *earlier), count, [(1, 0), (2, 3)])
    far_on = along(far, count, [(1, 0), (2, 3)])
    near = along(value, count, [(0, 1), (1, 0), (2, 3), (3, 2)])
    return [[value], [near], [middle, middle_on], [far, far_on]]


def sum_line(parts, count):
    done = ()

    def part(k):
        return parts[k](done) if callable(parts[k]) else parts[k]

    if count != 4:
        return [part(0)] + [shift(part(k), "seq", count, count - k) for k in range(1, count)]

    def joined(k):
        mine = part(k)
        other = along(mine, count, [(0, 1), (3, 2)])
        return (mine.astype(F32) + other.astype(F32)).astype(BF16), mine

    far, done_far = joined(3)
    done = (done_far,)
    middle, done_middle = joined(2)
    done = (done_middle,)
    near, mine = part(1), part(0)
    far_back = along(after(far, mine), count, [(2, 0), (1, 3)])
    middle_back = along(after(middle, mine), count, [(1, 2), (2, 1)])
    near_back = along(near, count, [(0, 1), (1, 0), (2, 3), (3, 2)])
    return [mine, near_back, middle_back, far_back]


def after(value, *earlier):
    return lax.optimization_barrier((value, *earlier))[0]


def gather_cube(block):
    mine = jnp.concatenate([block] + [flip(block, bits) for bits in (2, 4, 6)], axis=0)
    return [mine, flip(mine, 1)]


def length_of(where, lengths, slot_request):
    return lengths[slot_request[where[1]]]


def pack_kernel(count, heads, *refs):
    where, lengths, slot_request, tokens, gate, decay, logit = refs[:7]
    outs, (columns, edge, extra) = refs[7 : 7 + count], refs[7 + count :]
    me = where[0]
    piece, channels = tokens.shape
    block = channels // count
    heads_all = decay.shape[0]
    high = decay[...].astype(BF16)
    rest = decay[...] - high.astype(F32)
    middle = rest.astype(BF16)
    low = (rest - middle.astype(F32)).astype(BF16)
    for number, rows in enumerate((logit[...], high, middle, low)):
        columns[number * heads_all : (number + 1) * heads_all, :] = rows.astype(F32)
    first = length_of(where, lengths, slot_request) - (CONV - 1) - me * piece
    entry = lax.broadcasted_iota(jnp.int32, (8, piece), 0)
    spot = lax.broadcasted_iota(jnp.int32, (8, piece), 1)
    select = ((spot == first + entry) & (entry < CONV - 1)).astype(BF16)
    edge[...] = jnp.dot(select, tokens[...], preferred_element_type=F32)
    for k in range(count):
        target = lax.rem(me + k, count)
        start = target * heads

        def span(base, size):
            return pl.ds(pl.multiple_of(base + target * size, size), size)

        outs[k][:piece, : heads * DK] = tokens[:, span(0, heads * DK)]
        outs[k][:piece, heads * DK : 2 * heads * DK] = tokens[:, span(HK, heads * DK)]
        outs[k][:piece, 2 * heads * DK : block] = tokens[:, span(2 * HK, heads * DV)]
        outs[k][:piece, block:] = gate[:, span(0, heads * DV)]
        extra[...] = jnp.zeros(extra.shape, F32)
        for number in range(4):
            for h in range(heads):
                at = (number * heads + h) * piece
                extra[0:1, at : at + piece] = columns[pl.ds(number * heads_all + start + h, 1), :]
        extra[1:CONV, :] = edge[0 : CONV - 1, span(0, block)]
        outs[k][piece:, :block] = extra[...].astype(BF16)
        outs[k][piece:, block:] = jnp.zeros((16, heads * DV), BF16)


def pack(where, lengths, slot_request, tokens, gate, decay, logit, count):
    piece, channels = tokens.shape
    heads = HEADS // count
    block = channels // count
    return pl.pallas_call(
        functools.partial(pack_kernel, count, heads),
        out_shape=(jax.ShapeDtypeStruct((piece + 16, block + heads * DV), BF16),) * count,
        in_specs=[SMEM] * 3 + [VMEM] * 4,
        out_specs=(VMEM,) * count,
        scratch_shapes=[
            pltpu.VMEM((4 * HEADS, piece), F32),
            pltpu.VMEM((8, channels), F32),
            pltpu.VMEM((16, block), F32),
        ],
        name="pack",
    )(where, lengths, slot_request, tokens, gate, decay, logit)


def delta_kernel(count, heads, piece, *refs):
    x_refs, refs = refs[:count], refs[count:]
    where, lengths, slot_request, all_taps, gain, opened, state, xs, bs = refs
    me = where[0]
    length = length_of(where, lengths, slot_request)
    q0, k0, v0 = 0, heads * DK, 2 * heads * DK
    block = xs.shape[1]
    xs[pl.ds(0, 8), :] = jnp.zeros((8, block), F32)
    group = heads * piece
    lane = lax.broadcasted_iota(jnp.int32, (1, piece), 1)
    for k in range(count):
        c = lax.rem(me - k + count, count)
        at = pl.multiple_of(8 + c * piece, 8)
        xs[pl.ds(at, piece), :] = x_refs[k][:piece, :block].astype(F32)
        opened[c] = x_refs[k][:piece, block:]
        line = x_refs[k][piece:, :block].astype(F32)[0:1]
        strength = 1.0 / (1.0 + jnp.exp(-line[:, :group]))
        slope = line[:, group : 2 * group] + line[:, 2 * group : 3 * group] + line[:, 3 * group :]
        live = c * piece + lane < length
        for h in range(heads):
            span = slice(h * piece, (h + 1) * piece)
            bs[c, h : h + 1, :] = jnp.where(live, strength[:, span], 0.0)
            bs[c, heads + h : heads + h + 1, :] = jnp.where(live, slope[:, span], 0.0)
        bs[c, 2 * heads :, :] = jnp.zeros((8 - 2 * heads, piece), F32)

    def taps(i, col, width):
        base, step = (0, DK) if col < k0 else (HK, DK) if col < v0 else (2 * HK, DV)
        inside = col - (q0 if col < k0 else k0 if col < v0 else v0)
        at = pl.multiple_of(base + me * heads * step + inside, DK)
        return all_taps[i : i + 1, pl.ds(at, width)]

    def activated(c, col, width):
        total = None
        for i in range(CONV):
            rows = xs[pl.ds(8 - (CONV - 1) + i + c * piece, piece), pl.ds(col, width)]
            term = taps(i, col, width) * rows
            total = term if total is None else total + term
        return silu(total)

    def unit(v):
        return v * lax.rsqrt(jnp.sum(v * v, axis=-1, keepdims=True) + EPS_UNIT)

    row = lax.broadcasted_iota(jnp.int32, (piece, piece), 0)
    col = lax.broadcasted_iota(jnp.int32, (piece, piece), 1)
    upper = (row <= col).astype(F32)
    pairs = [(c, h) for c in range(count) for h in range(heads)]
    tabs = {}
    for c in range(count):
        rows = bs[c]
        cum = jnp.dot(rows, upper, precision=lax.Precision.HIGHEST, preferred_element_type=F32)
        wide = jnp.concatenate([cum, rows, jnp.zeros((piece - 16, piece), F32)], axis=0)
        tall = wide.T
        for h in range(heads):
            g_row = cum[heads + h : heads + h + 1, :]
            g_col = tall[:, heads + h : heads + h + 1]
            b_col = tall[:, 8 + h : 9 + h]
            tabs[c, h] = (g_row, g_col, b_col)
    couple, solve, first, second, ends = {}, {}, {}, {}, {}
    for c, h in pairs:
        g_row, g_col, b_col = tabs[c, h]
        q = unit(activated(c, q0 + h * DK, DK)) * DK ** (-0.5)
        k = unit(activated(c, k0 + h * DK, DK))
        v = activated(c, v0 + h * DV, DV)
        inner = dot_nt(jnp.concatenate([k, q], axis=0), k)
        spread = jnp.exp(jnp.where(row >= col, g_col - g_row, -1e30))
        couple[c, h] = jnp.where(row > col, inner[:piece] * spread * b_col, 0.0)
        grown = jnp.exp(g_col)
        g_end = g_row[:, piece - 1 : piece]
        to_end = jnp.exp(g_end - g_col) * k
        solve[c, h] = jnp.concatenate([b_col * v, (b_col * grown) * k], axis=1).astype(BF16)
        first[c, h] = (grown * q).astype(BF16)
        second[c, h] = jnp.concatenate([inner[piece:] * spread, to_end.T], axis=0).astype(BF16)
        ends[c, h] = jnp.exp(g_end)
    inverse = {}
    for p in pairs:
        inverse[p] = jnp.where(row == col, 1.0, 0.0) - jnp.where(
            (row >> 1) == (col >> 1), couple[p], 0.0
        )
    level = 1
    while (2 << level) <= piece:
        keep = ((row >> (level + 1)) == (col >> (level + 1))) & ((row >> level) != (col >> level))
        left = {p: dot(inverse[p], jnp.where(keep, couple[p], 0.0)) for p in pairs}
        for p in pairs:
            inverse[p] = inverse[p] - dot(left[p], inverse[p])
        level += 1
    solved = {p: dot(inverse[p], solve[p]) for p in pairs}
    running = [None] * heads
    for c in range(count):
        for h in range(heads):
            values, weighted = solved[c, h][:, :DV], solved[c, h][:, DV:]
            if c == 0:
                corrected = values
                out = None
            else:
                both = dot(
                    jnp.concatenate([weighted.astype(BF16), first[c, h]], axis=0), running[h]
                )
                corrected = values - both[:piece]
                out = both[piece:]
            both = dot(second[c, h], corrected)
            out = both[:piece] if out is None else out + both[:piece]
            running[h] = both[piece:] if c == 0 else ends[c, h] * running[h] + both[piece:]
            scale = lax.rsqrt(jnp.mean(out * out, axis=-1, keepdims=True) + EPS_NORM)
            span = slice(h * DV, (h + 1) * DV)
            gate = silu(opened[c, :, span].astype(F32))
            opened[c, :, span] = (out * scale * gain[...] * gate).astype(BF16)
    for h in range(heads):
        state[h] = running[h]


def delta(xs, where, lengths, slot_request, taps, gain, heads):
    count = len(xs)
    piece = xs[0].shape[0] - 16
    block = heads * (2 * DK + DV)
    return pl.pallas_call(
        functools.partial(delta_kernel, count, heads, piece),
        out_shape=(
            jax.ShapeDtypeStruct((count, piece, heads * DV), BF16),
            jax.ShapeDtypeStruct((heads, DK, DV), F32),
        ),
        in_specs=[VMEM] * count + [SMEM] * 3 + [VMEM] * 2,
        out_specs=(VMEM, VMEM),
        scratch_shapes=[
            pltpu.VMEM((8 + count * piece, block), F32),
            pltpu.VMEM((count, 8, piece), F32),
        ],
        compiler_params=pltpu.CompilerParams(vmem_limit_bytes=40 * MIB),
        cost_estimate=pl.CostEstimate(flops=int(4e9), bytes_accessed=4 * MIB, transcendentals=0),
        name="delta_rule",
    )(*xs, where, lengths, slot_request, taps, gain)


def project_kernel(count, orders, *refs):
    where, owners, mixed, refs = refs[0], refs[1], refs[2], refs[3:]
    parts, refs = refs[: len(orders)], refs[len(orders) :]
    outs, (weights, sems) = refs[:count], refs[count:]
    req = where[1]
    copies = []
    for j, (part, order) in enumerate(zip(parts, orders)):
        size = part.shape[0] // len(order or (0,))
        for i, bits in enumerate(order or (None,)):
            at = 0 if bits is None else pl.multiple_of((req ^ bits) * size, size)
            copies.append(
                pltpu.make_async_copy(
                    part.at[pl.ds(i * size, size), :], weights.at[pl.ds(at, size), :], sems.at[j, i]
                )
            )
            copies[-1].start()
    for copy in copies:
        copy.wait()
    for k in reversed(range(count)):
        outs[k][...] = jnp.dot(
            mixed[owners[k]], weights[...], preferred_element_type=F32
        ).astype(BF16)


def project(mixed, where, owners, parts):
    count, piece, depth = mixed.shape
    width = parts[0].shape[1]
    orders = [None] if len(parts) == 1 else [(0, 2, 4, 6), (1, 3, 5, 7)]
    return pl.pallas_call(
        functools.partial(project_kernel, count, orders),
        out_shape=(jax.ShapeDtypeStruct((piece, width), BF16),) * count,
        in_specs=[SMEM] * 2 + [VMEM] + [ANY] * len(parts),
        out_specs=(VMEM,) * count,
        scratch_shapes=[pltpu.VMEM((depth, width), BF16), pltpu.SemaphoreType.DMA((2, 4))],
        compiler_params=pltpu.CompilerParams(vmem_limit_bytes=24 * MIB),
        cost_estimate=pl.CostEstimate(
            flops=2 * count * piece * width * depth, bytes_accessed=4 * MIB, transcendentals=0
        ),
        name="output_projection",
    )(where, owners, mixed, *parts)


def norm_kernel(count, *refs):
    y_refs, (residual, gain, stream_out, normed_out) = refs[:count], refs[count:]
    total = y_refs[0][...].astype(F32)
    for y in y_refs[1:]:
        total += y[...].astype(F32)
    rounded = (residual[...].astype(F32) + total).astype(BF16)
    wide = rounded.astype(F32)
    scale = lax.rsqrt(jnp.mean(wide * wide, axis=-1, keepdims=True) + EPS_NORM)
    stream_out[...] = rounded
    normed_out[...] = (wide * scale * gain[...]).astype(BF16)


def norm(ys, residual, gain):
    count = len(ys)
    rows, width = residual.shape
    block = pl.BlockSpec((rows // 2, width), lambda i: (i, 0))
    return pl.pallas_call(
        functools.partial(norm_kernel, count),
        out_shape=(jax.ShapeDtypeStruct(residual.shape, BF16),) * 2,
        grid=(2,),
        in_specs=[block] * (count + 1) + [pl.BlockSpec((1, width), lambda i: (0, 0))],
        out_specs=(block, block),
        name="stream_norm",
    )(*ys, residual, gain)


def unflatten(refs, counts):
    refs = iter(refs)
    return [[next(refs) for _ in range(count)] for count in counts]


def forward_kernel(terms, shares, strips, *refs):
    x_refs, refs = refs[: sum(terms)], refs[sum(terms) :]
    early, weights, refs = refs[0], refs[1], refs[2:]
    count = len(terms)
    outs, (x, inner, spare, sems) = refs[:count], refs[count:]
    rows = x_refs[0].shape[0]
    depth = x.shape[1] // shares
    copies, spares = [], iter(range(sum(terms)))
    for k, arrays in enumerate(unflatten(x_refs, terms)):
        copies.append([])
        for i, array in enumerate(arrays):
            spot = next(spares)
            target = x.at[pl.ds(k * rows, rows), :] if i == 0 else spare.at[spot - k - 1]
            copy = pltpu.make_async_copy(array, target, sems.at[spot])
            copy.start()
            copies[k].append((copy, None if i == 0 else spot - k - 1))
    for k, group in enumerate(copies):
        for copy, spot in group:
            copy.wait()
            if spot is not None:
                x[k * rows : (k + 1) * rows, :] += spare[spot]

    half = depth // 2

    def product(which, start, size):
        total = None
        for r in range(shares):
            columns, low = slice(start, start + size), 5 * r * half
            if which == 0:
                rhs = weights[low : low + depth, columns]
            else:
                ahead = early[r * half : (r + 1) * half, columns]
                rest = weights[low + depth : low + depth + half, columns]
                rhs = jnp.concatenate([ahead, rest], axis=0)
            term = jnp.dot(
                x[:, r * depth : (r + 1) * depth], rhs, preferred_element_type=F32
            )
            total = term if total is None else total + term
        return total

    for start, size in strips:
        opened, upward = product(0, start, size), product(1, start, size)
        inner[:, start : start + size] = (silu(opened) * upward).astype(BF16)
    for r in range(shares):
        low = (5 * r + 3) * half
        term = dot_nt(inner[...], weights[low : low + depth, :]).astype(BF16)
        for k in range(count):
            outs[k][:, r * depth : (r + 1) * depth] = term[k * rows : (k + 1) * rows]


def forward(xs, early, weights, shares):
    rows, width = xs[0][0].shape
    count, hidden = len(xs), weights.shape[1]
    total = count * rows
    strips = [(start, min(STRIP, hidden - start)) for start in range(0, hidden, STRIP)]
    terms = [len(arrays) for arrays in xs]
    return pl.pallas_call(
        functools.partial(forward_kernel, terms, shares, strips),
        out_shape=(jax.ShapeDtypeStruct((rows, width), BF16),) * count,
        in_specs=[ANY] * sum(terms) + [VMEM] * 2,
        out_specs=(VMEM,) * count,
        scratch_shapes=[
            pltpu.VMEM((total, width), BF16),
            pltpu.VMEM((total, hidden), BF16),
            pltpu.VMEM((max(1, sum(terms) - count), rows, width), BF16),
            pltpu.SemaphoreType.DMA((sum(terms),)),
        ],
        compiler_params=pltpu.CompilerParams(vmem_limit_bytes=24 * MIB),
        cost_estimate=pl.CostEstimate(
            flops=6 * total * width * hidden, bytes_accessed=20 * MIB, transcendentals=0
        ),
        name="feed_forward",
    )(*sum(xs, []), early, weights)


def finish_kernel(count, *refs):
    y_refs, (where, lengths, slot_request, stream, out) = refs[:count], refs[count:]
    rows = stream.shape[0]
    start = (where[0] * pl.num_programs(0) + pl.program_id(0)) * rows
    position = start + lax.broadcasted_iota(jnp.int32, (rows, 1), 0)
    total = stream[...].astype(F32)
    for y in y_refs:
        total += y[...].astype(F32)
    live = position < length_of(where, lengths, slot_request)
    out[...] = jnp.where(live, total, 0.0).astype(BF16)


def finish(ys, where, lengths, slot_request, stream):
    count = len(ys)
    rows, width = stream.shape
    block = pl.BlockSpec((rows // 2, width), lambda i: (i, 0))
    return pl.pallas_call(
        functools.partial(finish_kernel, count),
        out_shape=jax.ShapeDtypeStruct(stream.shape, BF16),
        grid=(2,),
        in_specs=[block] * count + [SMEM] * 3 + [block],
        out_specs=block,
        name="last_sum",
    )(*ys, where, lengths, slot_request, stream)


def local(
    qkv_proj,
    gate_proj,
    residual,
    log_decay,
    beta_logit,
    lengths,
    slot_request,
    conv_weight,
    norm_gain,
    out_weight,
    mlp_gain,
    w_gate,
    w_up,
    w_down,
):
    me = lax.axis_index("seq")
    req = lax.axis_index("req")
    count = lax.axis_size("seq")
    n_req = lax.axis_size("req")
    piece = qkv_proj.shape[1]
    heads = HEADS // count
    where = jnp.stack([me, req]).astype(jnp.int32)

    packed = pack(
        where, lengths, slot_request, qkv_proj[0], gate_proj[0], log_decay[0].T, beta_logit[0].T, count
    )
    xs = [packed[0]] + [shift(packed[k], "seq", count, k) for k in range(1, count)]
    block = qkv_proj.shape[2] // count
    conv_edge = sum(x[piece + 1 : piece + CONV, :block].astype(F32) for x in xs).astype(BF16)

    placed = lax.ppermute(
        out_weight,
        ("req", "seq"),
        [(i, (i % n_req) * count + i // n_req) for i in range(n_req * count)],
    )
    if cubic():
        out_parts = gather_cube(placed)
    else:
        out_parts = [lax.all_gather(placed, "req", axis=0, tiled=True)]
    half = w_up.shape[0] // 2
    early = lax.all_gather(w_up[:half], "req", axis=0, tiled=True)
    weights = jnp.concatenate([w_gate, w_up[half:], w_down.T], axis=0)
    weights = after(weights, early, out_parts[0], *xs[1:])
    weights = lax.all_gather(weights, "req", axis=0, tiled=True)
    mixed, state = delta(xs, where, lengths, slot_request, conv_weight, norm_gain[None, :], heads)
    ys = project(mixed, where, owners_of(count), out_parts)
    stream, normed = norm(sum_line(ys, count), residual[0], mlp_gain[None, :])
    blocks = gather_line(normed, count, weights)
    first = min(2, count)
    nearest = []

    def near(k, done):
        if not nearest:
            nearest.extend(forward(after(blocks[:first], *done), early, weights, n_req))
        return nearest[k]

    def far(k, done):
        return forward(after([blocks[k]], *done, *blocks[first - 1]), early, weights, n_req)[0]

    parts = [functools.partial(near if k < first else far, k) for k in range(count)]
    hidden = finish(sum_line(parts, count), where, lengths, slot_request, stream)
    return hidden[None], state[None], conv_edge[None]


def solution(mesh):
    return jax.shard_map(
        local,
        mesh=mesh,
        in_specs=(
            P("req", "seq", None),
            P("req", "seq", None),
            P("req", "seq", None),
            P("req", "seq", None),
            P("req", "seq", None),
            P(),
            P(),
            P(),
            P(),
            P(("req", "seq"), None),
            P(),
            P("req", "seq"),
            P("req", "seq"),
            P("seq", "req"),
        ),
        out_specs=(P("req", "seq", None), P("req", "seq", None, None), P("req", None, "seq")),
        check_vma=False,
    )
```
